32 devices in a mesh: groups: 2 (over x), dp: 8 (over z, y), fsdp: 2 (over core).
Axes of the slice: x: 2, y: 2, z: 4, core: 2. Of those that a mesh axis runs over, the one named last changes fastest.
Arguments:
- hidden: bfloat16 [8192, 8192], P(('groups', 'dp', 'fsdp')), parts along dimension 0, may hold values from -600 to 600
- norm_gain: bfloat16 [8192], P('fsdp'), may hold values from 0.099609375 to 1.8984375
- w_query: bfloat16 [8192, 512], P('fsdp'), may hold values from -0.06629126 to 0.06629126
- w_key: bfloat16 [8192, 128], P('fsdp'), may hold values from -0.0625 to 0.0625
- w_value: bfloat16 [8192, 128], P('fsdp'), may hold values from -0.0625 to 0.0625
- b_query: bfloat16 [512], replicated, may hold values from -3 to 3
- b_key: bfloat16 [128], replicated, may hold values from -40 to 40
- b_value: bfloat16 [128], replicated, may hold values from -3 to 3
- row_host: int32 [8192], P(('groups', 'dp', 'fsdp')), parts along dimension 0, may hold values from 0 to 15, as said below
- row_slot: int32 [8192], P(('groups', 'dp', 'fsdp')), parts along dimension 0, may hold values from 0 to 7
Outputs:
- context: bfloat16 [8192, 512], P(('groups', 'dp', 'fsdp')), parts along dimension 0
The draws below stay inside these ranges and needn't reach their ends.
There are 2 independent parts, one for each index of `groups`. The reference program is written for one: setup_inputs(seed, part) draws one part's arguments, and reference() takes and returns one part's arrays. A program takes and returns all parts, laid end to end along the dimension named above; an argument that names none is the same for every part. Nothing has to cross between parts.
Inputs may be any that keep to these rules, and one draw needn't show every extreme that they name: `row_host`: index of the hosting device along dp and fsdp together. Of one device's rows at most 32 go to one host; in every draw some host receives exactly 32 rows from every device.
All inputs are finite; a program needn't handle non-finite values.
Results may differ from the reference program's by a relative error of at most 0.012.
The reference program's roundings to bfloat16 on the way count: a program that leaves them out, or rounds other values in their place, can miss the bound.
Values may be sent and summed in bfloat16 or wider, within the bound.
No kernel may reach another device: no remote copies, remote signals or barrier semaphores. Data moves between devices by JAX's collectives and lax.ppermute only.
A program may use at most 128 MiB of HBM per device.

```python
import math
import jax
import jax.numpy as jnp
from jax import lax

D = 8192
HD = 128
HQ = 4
TOK_DEV = 256
SEQ_HOST = 8
CAP = 32
RECV = 512
TOKENS = 4096


def layout(key):
    host_count = TOKENS // TOK_DEV
    half_cap = CAP // 2
    split_keys = jax.random.split(key, 5)
    target_host = jax.random.randint(split_keys[0], (), 0, host_count)
    host_index = jnp.arange(host_count)
    jitter = jax.random.randint(split_keys[1], (host_count, host_count), 0, 1 << 20)
    sort_score = jnp.where(host_index[None, :] == target_host, -1, jitter * host_count + host_index[None, :])
    ordering = jnp.argsort(sort_score, axis=1)
    amplitude = jax.random.randint(split_keys[2], (host_count, host_count // 2), 0, half_cap + 1)
    amplitude = amplitude.at[:, 0].set(half_cap)
    by_position = half_cap + jnp.stack([amplitude, -amplitude], axis=2).reshape(host_count, host_count)
    source_index = jnp.arange(host_count)[:, None]
    counts = jnp.zeros((host_count, host_count), jnp.int32).at[source_index, ordering].set(by_position)
    cumulative = jnp.cumsum(counts, axis=1)
    row_index = jnp.arange(TOK_DEV)
    labels = jnp.sum(cumulative[:, None, :] <= row_index[None, :, None], axis=2).astype(jnp.int32)
    shuffle_score = jax.random.randint(split_keys[3], (host_count, TOK_DEV), 0, 1 << 20) * TOK_DEV + row_index[None, :]
    shuffle = jnp.argsort(shuffle_score, axis=1)
    hosts_of_rows = jnp.take_along_axis(labels, shuffle, axis=1)
    same_host = hosts_of_rows[:, :, None] == hosts_of_rows[:, None, :]
    row_rank = jnp.sum(same_host & (row_index[None, None, :] < row_index[None, :, None]), axis=2)
    earlier = jnp.cumsum(counts, axis=0) - counts
    run_index = jnp.take_along_axis(earlier, hosts_of_rows, axis=1) + row_rank
    boundaries = jax.random.randint(split_keys[4], (host_count, SEQ_HOST - 1), 1, RECV)
    row_bounds = boundaries[hosts_of_rows]
    slots = jnp.sum(row_bounds <= run_index[:, :, None], axis=2)
    return (hosts_of_rows.reshape(TOKENS).astype(jnp.int32), slots.reshape(TOKENS).astype(jnp.int32))


def draw_row_host(key, part):
    return layout(key)[0]


def draw_row_slot(key, part):
    return layout(key)[1]


def draw_hidden(key, part):
    key = jax.random.fold_in(key, 11)
    split_keys = jax.random.split(key, 3)
    row_scale = jnp.exp(jax.random.uniform(split_keys[0], (TOKENS, 1), jnp.float32, 0.0, math.log(10.0)))
    column_scale = jnp.exp(jax.random.uniform(split_keys[1], (1, D), jnp.float32, 0.0, math.log(10.0)))
    result = jnp.clip(jax.random.normal(split_keys[2], (TOKENS, D), jnp.float32), -6.0, 6.0) * row_scale * column_scale
    return result.astype(jnp.bfloat16)


def draw_w_query(key, part):
    key = jax.random.fold_in(key, 12)
    fan_scale = D ** (-0.5)
    result = jnp.clip(jax.random.normal(key, (D, HQ * HD), jnp.float32), -6.0, 6.0) * fan_scale
    return result.astype(jnp.bfloat16)


def draw_b_key(key, part):
    key = jax.random.fold_in(key, 13)
    result = jnp.clip(jax.random.normal(key, (HD,), jnp.float32), -6.0, 6.0) * 0.5
    return result.astype(jnp.bfloat16)


def block_scale(rng, dims, shards, smallest, top_value):
    level = 1.0
    for axis_at, blocks in shards:
        heights = jax.random.uniform(jax.random.fold_in(jax.random.fold_in(rng, 6), axis_at), (blocks,), jnp.float32, smallest / len(shards), top_value / len(shards))
        level = level * jnp.repeat(jnp.exp(heights), dims[axis_at] // blocks).reshape((-1,) + (1,) * (len(dims) - 1 - axis_at))
    return level


def bell_draw(key, extent, spread, limit, cuts=(), kind=jnp.bfloat16):
    array = jax.random.normal(key, extent, jnp.float32) * spread
    if len(cuts) > 0:
        array = block_scale(key, extent, cuts, -0.22, 0.18) * array
    return jnp.clip(array, min=-limit, max=limit).astype(kind)


def setup_inputs(seed: int = 0, part: int = 0) -> dict:
    keys = jax.random.split(jax.random.key(seed), 11)
    part_keys = jax.random.split(jax.random.fold_in(keys[10], part), 11)
    return {
        "hidden": draw_hidden(jax.random.fold_in(jax.random.fold_in(keys[10], part), 71), part),
        "norm_gain": jnp.clip(1.0 + 0.18 * jax.random.normal(keys[1], (D,), jnp.float32), 0.099609375, 1.8984375).astype(jnp.bfloat16),
        "w_query": draw_w_query(jax.random.fold_in(keys[10], 71), part),
        "w_key": bell_draw(keys[3], (D, HD), D ** -0.5, 0.0625, ((0, 2),)),
        "w_value": bell_draw(keys[4], (D, HD), D ** -0.5, 0.0625, ((0, 2),)),
        "b_query": bell_draw(keys[5], (HQ * HD,), 0.5, 3.0),
        "b_key": draw_b_key(jax.random.fold_in(keys[10], 71), part),
        "b_value": bell_draw(keys[7], (HD,), 0.5, 3.0),
        "row_host": draw_row_host(jax.random.fold_in(jax.random.fold_in(keys[10], part), 71), part),
        "row_slot": draw_row_slot(jax.random.fold_in(jax.random.fold_in(keys[10], part), 71), part),
    }


rope_base = 1000000.0
epsilon = 1e-06

def rotary(tensor, position):
    half_dim = tensor.shape[-1] // 2
    frequency = jnp.power(rope_base, -jnp.arange(half_dim, dtype=jnp.float32) * 2.0 / tensor.shape[-1])
    rotation = position.astype(jnp.float32)[:, None] * frequency[None, :]
    cosine = jnp.cos(rotation)[:, None, :]
    sine_part = jnp.sin(rotation)[:, None, :]
    front_half = tensor[..., :half_dim]
    back_half = tensor[..., half_dim:]
    return jnp.concatenate([front_half * cosine - back_half * sine_part, back_half * cosine + front_half * sine_part], axis=-1)

def project_rows(block, norm_gain, w_query, w_key, w_value, b_query, b_key, b_value):
    widened = block.astype(jnp.float32)
    inverse = lax.rsqrt(lax.optimization_barrier(jnp.mean(widened * widened, axis=-1, keepdims=True)) + epsilon)
    normed = (widened * inverse * norm_gain.astype(jnp.float32)).astype(jnp.bfloat16)
    queries = (jnp.dot(normed, w_query, preferred_element_type=jnp.float32) + b_query.astype(jnp.float32)).astype(jnp.bfloat16)
    key_part = (jnp.dot(normed, w_key, preferred_element_type=jnp.float32) + b_key.astype(jnp.float32)).astype(jnp.bfloat16)
    value_part = (jnp.dot(normed, w_value, preferred_element_type=jnp.float32) + b_value.astype(jnp.float32)).astype(jnp.bfloat16)
    return jnp.concatenate([queries, key_part, value_part], axis=1)

def reference(hidden, norm_gain, w_query, w_key, w_value, b_query, b_key, b_value, row_host, row_slot):
    blocks = hidden.reshape(TOKENS // TOK_DEV, TOK_DEV, D)

    def project_block(block):
        return project_rows(block, norm_gain, w_query, w_key, w_value, b_query, b_key, b_value)
    projected = lax.map(project_block, blocks).reshape(TOKENS, (HQ + 2) * HD)
    sequence_key = (row_host * SEQ_HOST + row_slot).astype(jnp.int32)
    ordering = jnp.argsort(sequence_key, stable=True).astype(jnp.int32)
    sorted_key = sequence_key[ordering]
    index_row = jnp.arange(TOKENS, dtype=jnp.int32)
    is_first = jnp.concatenate([jnp.ones((1,), bool), sorted_key[1:] != sorted_key[:-1]])
    starts = jnp.where(is_first, index_row, jnp.zeros_like(index_row))
    position = index_row - lax.cummax(starts)
    arranged = projected[ordering]
    query_width = HQ * HD
    query_rot = rotary(arranged[:, :query_width].reshape(TOKENS, HQ, HD).astype(jnp.float32), position).astype(jnp.bfloat16)
    key_rot = rotary(arranged[:, query_width:query_width + HD].astype(jnp.float32)[:, None, :], position)[:, 0, :].astype(jnp.bfloat16)
    values_all = arranged[:, query_width + HD:]
    key_pad = jnp.concatenate([jnp.zeros((RECV, HD), jnp.bfloat16), key_rot], axis=0)
    value_pad = jnp.concatenate([jnp.zeros((RECV, HD), jnp.bfloat16), values_all], axis=0)
    sequence_pad = jnp.concatenate([jnp.full((RECV,), -1, jnp.int32), sorted_key], axis=0)

    def block_attention(number):
        first_row = (number * RECV).astype(jnp.int32)
        query_block = lax.dynamic_slice_in_dim(query_rot, first_row, RECV, 0)
        key_block = lax.dynamic_slice_in_dim(key_pad, first_row, 2 * RECV, 0)
        value_block = lax.dynamic_slice_in_dim(value_pad, first_row, 2 * RECV, 0)
        sequence_block = lax.dynamic_slice_in_dim(sequence_pad, first_row, 2 * RECV, 0)
        query_sequence = lax.dynamic_slice_in_dim(sorted_key, first_row, RECV, 0)
        query_index = first_row + jnp.arange(RECV, dtype=jnp.int32)
        key_index = first_row - RECV + jnp.arange(2 * RECV, dtype=jnp.int32)
        allowed = (query_sequence[:, None] == sequence_block[None, :]) & (key_index[None, :] <= query_index[:, None])
        scores = jnp.einsum('qhd,kd->hqk', query_block.astype(jnp.float32), key_block.astype(jnp.float32)) * HD ** (-0.5)
        scores = jnp.where(allowed[None, :, :], scores, -jnp.inf)
        largest = lax.optimization_barrier(jnp.max(scores, axis=-1, keepdims=True))
        exponent = jnp.exp(scores - largest)
        attention = (exponent / lax.optimization_barrier(jnp.sum(exponent, axis=-1, keepdims=True))).astype(jnp.bfloat16)
        context = jnp.einsum('hqk,kd->qhd', attention.astype(jnp.float32), value_block.astype(jnp.float32))
        return context.astype(jnp.bfloat16).reshape(RECV, query_width)
    block_outputs = lax.map(block_attention, jnp.arange(TOKENS // RECV, dtype=jnp.int32))
    sorted_context = block_outputs.reshape(TOKENS, query_width)
    return jnp.zeros_like(sorted_context).at[ordering].set(sorted_context)
```

```python
import functools
import jax
import jax.numpy as jnp
from jax import lax
from jax.experimental import pallas as pl
from jax.experimental.pallas import tpu as pltpu
from jax.sharding import PartitionSpec as P

HD = 128
HQ = 4
QW = HQ * HD
SLOTS_PER_HOST = 8
BLOCK = 32
rope_base = 1000000.0
epsilon = 1e-06
f32 = jnp.float32
bf16 = jnp.bfloat16
MIB = 1024 * 1024


def params(mib=40):
    return pltpu.CompilerParams(vmem_limit_bytes=mib * MIB)


def norm_kernel(core_ref, hidden_ref, gain_ref, wk_ref, wv_ref, own_ref, other_ref, pk_ref, pv_ref):
    step = pl.program_id(0)
    rows, width = hidden_ref.shape
    half = width // 2
    here = pl.multiple_of(step * rows, rows)
    core = core_ref[0]
    wide = hidden_ref[...].astype(f32)
    inverse = lax.rsqrt(jnp.sum(wide * wide, axis=1, keepdims=True) * (1.0 / width) + epsilon)

    def normed(part, gain_row):
        start = pl.multiple_of(part * half, half)
        block = hidden_ref[:, pl.ds(start, half)].astype(f32)
        return (block * inverse * gain_ref[gain_row : gain_row + 1, :].astype(f32)).astype(bf16)

    own_ref[pl.ds(here, rows), :] = normed(core, 0)
    other_ref[pl.ds(here, rows), :] = normed(1 - core, 1)

    @pl.when(step == pl.num_programs(0) - 1)
    def _():
        own = own_ref[...]
        pk_ref[...] = jnp.dot(own, wk_ref[...], preferred_element_type=f32)
        pv_ref[...] = jnp.dot(own, wv_ref[...], preferred_element_type=f32)


def norm_and_own_half(core, hidden, gains, w_key, w_value):
    rows, width = hidden.shape
    half = width // 2
    block = 32
    whole = lambda shape: pl.BlockSpec(shape, lambda i, c: (0, 0))
    return pl.pallas_call(
        norm_kernel,
        grid_spec=pltpu.PrefetchScalarGridSpec(
            num_scalar_prefetch=1,
            grid=(rows // block,),
            in_specs=[
                pl.BlockSpec((block, width), lambda i, c: (i, 0)),
                whole((2, half)),
                whole((half, HD)),
                whole((half, HD)),
            ],
            out_specs=[
                whole((rows, half)),
                whole((rows, half)),
                whole((rows, HD)),
                whole((rows, HD)),
            ],
        ),
        out_shape=[
            jax.ShapeDtypeStruct((rows, half), bf16),
            jax.ShapeDtypeStruct((rows, half), bf16),
            jax.ShapeDtypeStruct((rows, HD), f32),
            jax.ShapeDtypeStruct((rows, HD), f32),
        ],
        compiler_params=params(),
        name="norm_own_half",
    )(core, hidden, gains, w_key, w_value)


def rotate(block, cosine, sine):
    turned = jnp.concatenate([block[:, HD // 2 :], block[:, : HD // 2]], axis=1)
    return block * cosine + turned * sine


def key_value_kernel(other_ref, wk_ref, wv_ref, pk_ref, pv_ref, bk_ref, bv_ref, cos_ref, sin_ref, out_ref):
    other = other_ref[...]
    keys = pk_ref[...] + jnp.dot(other, wk_ref[...], preferred_element_type=f32)
    keys = (keys + bk_ref[...].astype(f32)).astype(bf16).astype(f32)
    out_ref[:, :HD] = rotate(keys, cos_ref[...], sin_ref[...]).astype(bf16)
    values = pv_ref[...] + jnp.dot(other, wv_ref[...], preferred_element_type=f32)
    out_ref[:, HD:] = (values + bv_ref[...].astype(f32)).astype(bf16)


def keys_and_values(other, w_key, w_value, part_key, part_value, b_key, b_value, cosine, sine):
    rows = other.shape[0]
    return pl.pallas_call(
        key_value_kernel,
        out_shape=jax.ShapeDtypeStruct((rows, 2 * HD), bf16),
        compiler_params=params(),
        name="keys_values",
    )(other, w_key, w_value, part_key, part_value, b_key[None], b_value[None], cosine, sine)


def query_kernel(own_ref, other_ref, w_own_ref, w_other_ref, b_ref, cos_ref, sin_ref, out_ref):
    total = jnp.dot(own_ref[...], w_own_ref[...], preferred_element_type=f32)
    total += jnp.dot(other_ref[...], w_other_ref[...], preferred_element_type=f32)
    total = (total + b_ref[...].astype(f32)).astype(bf16).astype(f32)
    cosine = cos_ref[...]
    sine = sin_ref[...]
    for head in range(HQ):
        at = slice(head * HD, (head + 1) * HD)
        out_ref[:, at] = rotate(total[:, at], cosine, sine).astype(bf16)


def queries_of(own, other, w_own, w_other, b_query, cosine, sine):
    rows = own.shape[0]
    return pl.pallas_call(
        query_kernel,
        out_shape=jax.ShapeDtypeStruct((rows, QW), bf16),
        compiler_params=params(),
        name="queries",
    )(own, other, w_own, w_other, b_query[None], cosine, sine)


def one_hot(slot_row, slots):
    rows = slot_row.shape[1]
    at = lax.broadcasted_iota(jnp.int32, (slots, rows), 0)
    return jnp.where(at == slot_row, 1.0, 0.0).astype(bf16)


def attention_kernel(counts, q_ref, slot_ref, key_seq_ref, query_seq_ref, *rest):
    piece_refs = rest[: len(counts)]
    out_ref, keys, values, contexts = rest[len(counts) :]
    blocks = keys.shape[0]
    slots = blocks * BLOCK

    def spread(piece, index):
        hot = one_hot(slot_ref[pl.ds(index, 1), :], slots)
        rows = jnp.dot(hot, piece, preferred_element_type=f32).astype(bf16)
        rows = rows.reshape(blocks, BLOCK, 2 * HD)
        at = pl.ds(pl.multiple_of(index * BLOCK, BLOCK), BLOCK)
        keys[:, at, :] = rows[:, :, :HD]
        values[:, at, :] = rows[:, :, HD:]

    first = 0
    for ref, count in zip(piece_refs, counts):
        if count == 1:
            spread(ref[...], first)
        else:
            lax.fori_loop(0, count, lambda i, c: (spread(ref[i], first + i), c)[1], 0)
        first += count
    total = first * BLOCK

    own_hot = one_hot(slot_ref[first : first + 1, :], slots)
    q_slots = jnp.dot(own_hot, q_ref[...], preferred_element_type=f32).astype(bf16)
    own_at = key_seq_ref[blocks : blocks + 1, :]
    q_index = lax.broadcasted_iota(jnp.int32, (HQ * BLOCK, total), 0) % BLOCK
    ordered = own_at <= q_index
    for block in range(blocks):
        rows = slice(block * BLOCK, (block + 1) * BLOCK)
        q_block = q_slots[rows, :]
        q_heads = jnp.concatenate([q_block[:, h * HD : (h + 1) * HD] for h in range(HQ)], axis=0)
        scores = lax.dot_general(
            q_heads, keys[block], (((1,), (1,)), ((), ())), preferred_element_type=f32
        ) * HD ** (-0.5)
        q_seq = query_seq_ref[rows, :]
        q_seq = jnp.concatenate([q_seq] * HQ, axis=0)
        allowed = (key_seq_ref[block : block + 1, :] == q_seq) & ordered
        scores = jnp.where(allowed, scores, -1e30)
        exponent = jnp.exp(scores - jnp.max(scores, axis=1, keepdims=True))
        weights = (exponent / jnp.sum(exponent, axis=1, keepdims=True)).astype(bf16)
        context = jnp.dot(weights, values[block], preferred_element_type=f32).astype(bf16)
        for h in range(HQ):
            contexts[rows, h * HD : (h + 1) * HD] = context[h * BLOCK : (h + 1) * BLOCK, :]
    out_ref[...] = lax.dot_general(
        own_hot, contexts[...], (((0,), (0,)), ((), ())), preferred_element_type=f32
    ).astype(bf16)


def attend(queries, slots_of_rows, key_seq, query_seq, pieces):
    rows = queries.shape[0]
    counts = tuple(1 if p.ndim == 2 else p.shape[0] for p in pieces)
    blocks = key_seq.shape[0] - 1
    total = key_seq.shape[1]
    return pl.pallas_call(
        functools.partial(attention_kernel, counts),
        out_shape=jax.ShapeDtypeStruct((rows, QW), bf16),
        scratch_shapes=[
            pltpu.VMEM((blocks, total, HD), bf16),
            pltpu.VMEM((blocks, total, HD), bf16),
            pltpu.VMEM((blocks * BLOCK, QW), bf16),
        ],
        compiler_params=params(56),
        name="attention",
    )(queries, slots_of_rows, key_seq, query_seq, *pieces)


def swap_cores(array):
    return lax.ppermute(array, "fsdp", [(0, 1), (1, 0)])


def far(array, shift, near):
    count = lax.axis_size("dp")
    return lax.ppermute(array, "dp", [(i, (i + shift * near) % count) for i in range(count)])


def swap_near(array):
    count = lax.axis_size("dp")
    return lax.ppermute(array, "dp", [(i, i ^ 1) for i in range(count)])


def stepped():
    return lax.axis_size("dp") == 8


def gather_pieces(array):
    line = [array] + [far(array, shift, 2) for shift in range(1, lax.axis_size("dp") // 2)]
    plane = line + [swap_near(a) for a in line]
    return plane + [swap_cores(a) for a in plane]


def gather_small(array):
    line = jnp.stack([array] + [far(array, shift, 2) for shift in range(1, lax.axis_size("dp") // 2)])
    plane = jnp.concatenate([line, swap_near(line)])
    return jnp.concatenate([plane, swap_cores(plane)])


def piece_sources():
    count = lax.axis_size("dp")
    row, core = lax.axis_index("dp"), lax.axis_index("fsdp")
    far_count = count // 2
    line = (((row // 2) - jnp.arange(far_count)) % far_count) * 2 + row % 2
    plane = jnp.concatenate([line, line ^ 1])
    return jnp.concatenate([plane * 2 + core, plane * 2 + 1 - core])


def per_device(
    hidden, norm_gain, w_query, w_key, w_value, b_query, b_key, b_value, row_host, row_slot
):
    host_count = lax.axis_size(("dp", "fsdp"))
    rows = hidden.shape[0]
    capacity = 2 * rows // host_count
    slots = host_count * capacity
    blocks = slots // BLOCK
    seq_count = host_count * SLOTS_PER_HOST
    core = lax.axis_index("fsdp")
    me = lax.axis_index(("dp", "fsdp"))

    index_row = jnp.arange(rows)
    lower = index_row[None, :] < index_row[:, None]
    same_host = row_host[:, None] == row_host[None, :]
    seq = row_host * SLOTS_PER_HOST + row_slot
    same_seq = seq[:, None] == seq[None, :]
    row_rank = jnp.sum(same_host & lower, axis=1, dtype=jnp.int32)
    seq_rank = jnp.sum(same_seq & lower, axis=1, dtype=jnp.int32)
    slot_index = row_host * capacity + row_rank
    slot_hot = slot_index[None, :] == jnp.arange(slots)[:, None]
    seq_of_slot = jnp.max(jnp.where(slot_hot, seq[None, :], -1), axis=1)
    seq_hot = seq[:, None] == jnp.arange(seq_count)[None, :]
    seq_size = jnp.sum(seq_hot, axis=0, dtype=jnp.int32)

    small = jnp.concatenate([slot_index, seq_of_slot, seq_size])
    if stepped():
        small_all = gather_small(small)
        sources = piece_sources()
    else:
        small_all = lax.all_gather(small, ("dp", "fsdp"))
        sources = jnp.arange(host_count)
    piece_slots = small_all[:, :rows]
    earlier = sources < me
    own = sources == me
    base = jnp.sum(jnp.where(earlier[:, None], small_all[:, rows + slots :], 0), axis=0)
    position = seq_rank + jnp.sum(jnp.where(seq_hot, base[None, :], 0), axis=1)
    key_seq = jnp.where((sources <= me)[:, None], small_all[:, rows : rows + slots], -1)
    key_seq = key_seq.reshape(host_count, blocks, BLOCK).transpose(1, 0, 2).reshape(blocks, -1)
    own_at = jnp.where(own[:, None], jnp.arange(BLOCK)[None, :], -1).reshape(1, -1)
    key_seq = jnp.concatenate([key_seq, own_at])
    query_seq = jnp.where(seq_of_slot < 0, -2, seq_of_slot)[:, None]
    slots_of_rows = jnp.concatenate([piece_slots, slot_index[None]])

    frequency = jnp.power(rope_base, -jnp.arange(HD // 2, dtype=f32) * 2.0 / HD)
    rotation = position.astype(f32)[:, None] * frequency[None, :]
    cosine, sine = jnp.cos(rotation), jnp.sin(rotation)
    cosine = jnp.concatenate([cosine, cosine], axis=1)
    sine = jnp.concatenate([-sine, sine], axis=1)

    gain_other = swap_cores(norm_gain)
    w_value_other = swap_cores(w_value)
    w_key_other = swap_cores(w_key)
    w_query_other = swap_cores(w_query)
    gains = jnp.stack([norm_gain, gain_other])
    own_half, other_half, part_key, part_value = norm_and_own_half(
        core.reshape(1), hidden, gains, w_key, w_value
    )
    pairs = keys_and_values(
        other_half, w_key_other, w_value_other, part_key, part_value, b_key, b_value, cosine, sine
    )
    if stepped():
        pieces = gather_pieces(pairs)
    else:
        pieces = [lax.all_gather(pairs, ("dp", "fsdp"))]
    queries = queries_of(own_half, other_half, w_query, w_query_other, b_query, cosine, sine)
    return attend(queries, slots_of_rows, key_seq, query_seq, pieces)


def solution(mesh):
    return jax.shard_map(
        per_device,
        mesh=mesh,
        in_specs=(
            P(("groups", "dp", "fsdp"), None),
            P("fsdp"),
            P("fsdp", None),
            P("fsdp", None),
            P("fsdp", None),
            P(),
            P(),
            P(),
            P(("groups", "dp", "fsdp")),
            P(("groups", "dp", "fsdp")),
        ),
        out_specs=P(("groups", "dp", "fsdp"), None),
        check_vma=False,
    )
```

```python
import functools
import jax
import jax.numpy as jnp
import numpy as np
from jax import lax
from jax.experimental import pallas as pl
from jax.experimental.pallas import tpu as pltpu
from jax.sharding import PartitionSpec as P

HD = 128
HQ = 4
QW = HQ * HD
SLOTS_PER_HOST = 8
BLOCK = 32
LARGE = 1e30
FACTS = 16
KV_MIB = 56
rope_base = 1000000.0
epsilon = 1e-06
f32 = jnp.float32
bf16 = jnp.bfloat16
i32 = jnp.int32
MIB = 1024 * 1024
ANYWHERE = pl.BlockSpec(memory_space=pltpu.HBM)


def params(mib=58):
    return pltpu.CompilerParams(vmem_limit_bytes=mib * MIB)


def whole(shape):
    return pl.BlockSpec(shape, lambda *i: (0,) * len(shape))


def rotary_table(positions):
    frequency = np.power(np.float32(rope_base), -np.arange(HD // 2, dtype=np.float32) * np.float32(2.0 / HD))
    rotation = np.arange(positions, dtype=np.float32)[:, None] * frequency.astype(np.float32)[None, :]
    rotation = rotation.astype(np.float64)
    rest = np.concatenate([np.cos(rotation), np.sin(rotation)], axis=1).astype(np.float32)
    terms = []
    for _ in range(2):
        term = rest.astype(jnp.bfloat16)
        terms.append(term)
        rest = rest - term.astype(np.float32)
    return np.concatenate(terms, axis=1)


def key_value_kernel(core_ref, gain_other_ref, hidden_hbm, *rest):
    weights_hbm, small_hbm, rest = rest[:4], rest[4:9], rest[9:]
    out_ref, normed_hbm, hidden, normed, gains, wk, wv, wk_other, wv_other, *rest = rest
    small, (in_sems, sems, out_sems) = rest[:5], rest[5:]
    gain_ref, bk_ref, bv_ref, host_ref, slot_ref = small
    rows, width = hidden.shape
    half = width // 2
    core = core_ref[0]
    own_at = pl.multiple_of(core * half, half)
    other_at = pl.multiple_of((1 - core) * half, half)
    parts = in_sems.shape[0]
    part_rows = rows // parts
    lanes = 1024
    high = 8

    small_copies = [pltpu.make_async_copy(a, b, sems.at[4 + i]) for i, (a, b) in enumerate(zip(small_hbm, small))]
    weights = (wk, wv, wk_other, wv_other)
    weight_copies = [pltpu.make_async_copy(a, b, sems.at[i]) for i, (a, b) in enumerate(zip(weights_hbm, weights))]

    def span(i):
        return pl.ds(i * part_rows, part_rows)

    loads = [pltpu.make_async_copy(hidden_hbm.at[span(i), :], hidden.at[span(i), :], in_sems.at[i]) for i in range(parts)]
    saves = [pltpu.make_async_copy(normed.at[span(i), :], normed_hbm.at[span(i), :], out_sems.at[i]) for i in range(parts)]
    for c in small_copies + loads + weight_copies:
        c.start()
    for c in small_copies:
        c.wait()
    gains[:, pl.ds(own_at, half)] = jnp.broadcast_to(gain_ref[...].astype(f32)[None, :], (high, half))
    gains[:, pl.ds(other_at, half)] = jnp.broadcast_to(gain_other_ref[...].astype(f32)[None, :], (high, half))
    tail = out_ref.shape[0] - rows
    line = lax.broadcasted_iota(i32, (tail, rows), 0)
    facts = jnp.where(line == 0, host_ref[...][None, :], jnp.where(line == 1, slot_ref[...][None, :], 0))
    out_ref[rows:, :] = facts.astype(f32).astype(bf16)

    for i in range(parts):
        at = slice(i * part_rows, (i + 1) * part_rows)
        loads[i].wait()
        total = jnp.zeros((part_rows, lanes), f32)
        for j in range(width // lanes):
            wide = hidden[at, j * lanes : (j + 1) * lanes].astype(f32)
            total += wide * wide
        mean = jnp.sum(total, axis=1, keepdims=True) * (1.0 / width)
        scale = lax.rsqrt(mean + epsilon)
        for j in range(width // lanes):
            to = slice(j * lanes, (j + 1) * lanes)
            wide = (hidden[at, to].astype(f32) * scale).reshape(part_rows // high, high, lanes)
            normed[at, to] = (wide * gains[:, to][None]).reshape(part_rows, lanes).astype(bf16)
        saves[i].start()
    for c in weight_copies[:2]:
        c.wait()
    total = jnp.dot(
        normed[:, pl.ds(own_at, half)], jnp.concatenate([wk[...], wv[...]], axis=1), preferred_element_type=f32
    )
    for c in weight_copies[2:]:
        c.wait()
    total += jnp.dot(
        normed[:, pl.ds(other_at, half)],
        jnp.concatenate([wk_other[...], wv_other[...]], axis=1),
        preferred_element_type=f32,
    )
    out_ref[:rows, :HD] = (total[:, :HD] + bk_ref[...].astype(f32)[None, :]).astype(bf16)
    out_ref[:rows, HD:] = (total[:, HD:] + bv_ref[...].astype(f32)[None, :]).astype(bf16)
    for c in saves:
        c.wait()


def keys_and_values(core, gain_other, hidden, w_key, w_value, wk_other, wv_other, *small):
    rows, width = hidden.shape
    half = width // 2
    parts = 8
    vmem = pl.BlockSpec(memory_space=pltpu.VMEM)
    return pl.pallas_call(
        key_value_kernel,
        in_specs=[pl.BlockSpec(memory_space=pltpu.SMEM), vmem] + [ANYWHERE] * (5 + len(small)),
        out_specs=[vmem, ANYWHERE],
        out_shape=[
            jax.ShapeDtypeStruct((rows + FACTS, 2 * HD), bf16),
            jax.ShapeDtypeStruct((rows, width), bf16),
        ],
        scratch_shapes=[
            pltpu.VMEM((rows, width), bf16),
            pltpu.VMEM((rows, width), bf16),
            pltpu.VMEM((8, width), f32),
            *[pltpu.VMEM((half, HD), bf16)] * 4,
            *[pltpu.VMEM(a.shape, a.dtype) for a in small],
            pltpu.SemaphoreType.DMA((parts,)),
            pltpu.SemaphoreType.DMA((4 + len(small),)),
            pltpu.SemaphoreType.DMA((parts,)),
        ],
        compiler_params=params(KV_MIB),
        cost_estimate=pl.CostEstimate(flops=8 * rows * half * HD, bytes_accessed=10 * MIB, transcendentals=0),
        name="keys_values",
    )(core, gain_other, hidden, w_key, w_value, wk_other, wv_other, *small)


def query_kernel(mine, core_ref, rows_hbm, weights_hbm, *rest):
    if mine:
        out_ref, rows, weights, sems = rest
    else:
        sum_hbm, b_hbm, out_ref, rows, weights, total_ref, b_ref, sems = rest
    half = weights.shape[0]
    parts = 4
    chunk = half // parts
    side = core_ref[0] if mine else 1 - core_ref[0]
    copies = []
    for i in range(parts):
        at = pl.ds(i * chunk, chunk)
        source = pl.ds(pl.multiple_of(side * half + i * chunk, chunk), chunk)
        copies.append(pltpu.make_async_copy(rows_hbm.at[:, source], rows.at[:, at], sems.at[2 * i]))
        copies.append(pltpu.make_async_copy(weights_hbm.at[at, :], weights.at[at, :], sems.at[2 * i + 1]))
    if not mine:
        copies.append(pltpu.make_async_copy(sum_hbm, total_ref, sems.at[2 * parts]))
        copies.append(pltpu.make_async_copy(b_hbm, b_ref, sems.at[2 * parts + 1]))
    for c in copies:
        c.start()
    total = None
    for i in range(parts):
        copies[2 * i].wait()
        copies[2 * i + 1].wait()
        at = slice(i * chunk, (i + 1) * chunk)
        here = jnp.dot(rows[:, at], weights[at, :], preferred_element_type=f32)
        total = here if total is None else total + here
    if mine:
        out_ref[...] = total
    else:
        copies[-2].wait()
        copies[-1].wait()
        out_ref[...] = (total + total_ref[...] + b_ref[...].astype(f32)[None, :]).astype(bf16)


def query_half(mine, core, normed, weights, *more):
    rows = normed.shape[0]
    half = weights.shape[0]
    extra = [] if mine else [pltpu.VMEM((rows, QW), f32), pltpu.VMEM((QW,), bf16)]
    return pl.pallas_call(
        functools.partial(query_kernel, mine),
        in_specs=[pl.BlockSpec(memory_space=pltpu.SMEM)] + [ANYWHERE] * (2 + len(more)),
        out_shape=jax.ShapeDtypeStruct((rows, QW), f32 if mine else bf16),
        scratch_shapes=[
            pltpu.VMEM((rows, half), bf16),
            pltpu.VMEM((half, QW), bf16),
            *extra,
            pltpu.SemaphoreType.DMA((10,)),
        ],
        compiler_params=params(KV_MIB),
        cost_estimate=pl.CostEstimate(flops=2 * rows * half * QW, bytes_accessed=6 * MIB, transcendentals=0),
        name="queries_own" if mine else "queries_other",
    )(core, normed, weights, *more)


class Group:
    def __init__(self, pieces, rows, capacity, seq_count, lower_ref, usable_ref, before_count, first):
        self.pieces = pieces
        count = len(pieces)
        shift = SLOTS_PER_HOST.bit_length() - 1
        facts = [p[rows:, :].astype(f32) for p in pieces]
        hosts = jnp.concatenate([f[0:1] for f in facts], axis=0).astype(i32)
        seqs = hosts * SLOTS_PER_HOST + jnp.concatenate([f[1:2] for f in facts], axis=0).astype(i32)
        padded = jnp.concatenate([seqs, jnp.zeros((HD - count, rows), i32)], axis=0)
        columns = jnp.transpose(padded.astype(f32)).astype(i32)
        at_row = lax.broadcasted_iota(i32, (rows, rows), 0)
        at_lane = lax.broadcasted_iota(i32, (rows, rows), 1)
        before = jnp.where(at_row < at_lane, 1, 0)
        below = jnp.where(at_lane < at_row, 1.0, 0.0).astype(bf16)
        seq_lanes = lax.broadcasted_iota(i32, (rows, seq_count), 1)
        code_lanes = lax.broadcasted_iota(i32, (rows, HD), 1)
        codes_in_block = SLOTS_PER_HOST * BLOCK // capacity
        hots, counts, self.slots, self.marks = [], [], [], []
        for p in range(count):
            column = columns[:, p : p + 1]
            hot = jnp.where(seq_lanes == column, 1.0, 0.0)
            hots.append(hot)
            counts.append(jnp.sum(hot, axis=0, keepdims=True))
            same = lax.shift_right_logical(column, shift) == hosts[p : p + 1, :]
            rank = jnp.sum(jnp.where(same, before, 0), axis=0, keepdims=True)
            self.slots.append(hosts[p : p + 1, :] * capacity + rank)
            code = jnp.where(usable_ref[first + p] > 0, lax.bitwise_and(column, codes_in_block - 1), -1)
            mark = (code_lanes == code) | ((code_lanes == HD - 1) & (code >= 0))
            self.marks.append(jnp.where(mark, 1.0, 0.0).astype(bf16))
        base = jnp.zeros((count, seq_count), f32) + before_count
        for q in range(count):
            base = base + lower_ref[first : first + count, first + q : first + q + 1] * counts[q]
        self.positions = []
        ranks = jnp.dot(below, jnp.concatenate(hots, axis=1).astype(bf16), preferred_element_type=f32)
        for p in range(count):
            earlier = ranks[:, p * seq_count : (p + 1) * seq_count] + base[p : p + 1, :]
            self.positions.append(jnp.sum(hots[p] * earlier, axis=1, keepdims=True).astype(i32))
        self.count = before_count
        for q in range(count):
            self.count = self.count + jnp.where(usable_ref[first + q] > 0, counts[q], 0.0)

    def turns(self, table):
        position = jnp.concatenate(self.positions, axis=0)
        places = lax.broadcasted_iota(i32, (position.shape[0], table.shape[0]), 1)
        hot = jnp.where(places == position, 1.0, 0.0).astype(bf16)
        terms = jnp.dot(hot, table[...], preferred_element_type=f32)
        return terms[:, :HD] + terms[:, HD:]


def turned(block, turn):
    half = HD // 2
    first = lax.broadcasted_iota(i32, block.shape, 1) < half
    other_turn = pltpu.roll(turn, half, 1)
    cosine = jnp.where(first, turn, other_turn)
    sine = jnp.where(first, -other_turn, turn)
    return block * cosine + pltpu.roll(block, half, 1) * sine


def one_hot(slot_row, slots):
    rows = slot_row.shape[1]
    at = lax.broadcasted_iota(i32, (slots, rows), 0)
    return jnp.where(at == slot_row, 1.0, 0.0).astype(bf16)


def spread_group(group, rows, table, keys, values, at_piece):
    blocks = keys.shape[0]
    slots = blocks * BLOCK
    last = lax.broadcasted_iota(i32, (slots, HD), 1) == HD - 1
    turns = group.turns(table)
    raw = jnp.concatenate([piece[:rows, :HD] for piece in group.pieces], axis=0)
    own_keys = turned(raw.astype(f32), turns).astype(bf16)
    for p, piece in enumerate(group.pieces):
        hot = one_hot(group.slots[p], slots)
        at = slice((at_piece + p) * BLOCK, (at_piece + p + 1) * BLOCK)
        both = jnp.concatenate([own_keys[p * rows : (p + 1) * rows], group.marks[p], piece[:rows, HD:]], axis=1)
        moved = jnp.dot(hot, both, preferred_element_type=f32)
        marks = moved[:, HD : 2 * HD]
        marks = jnp.where(last, 1.0 - marks, marks)
        keys[:, at, :HD] = moved[:, :HD].astype(bf16).reshape(blocks, BLOCK, HD)
        keys[:, at, HD:] = marks.astype(bf16).reshape(blocks, BLOCK, HD)
        values[:, at, :] = moved[:, 2 * HD :].astype(bf16).reshape(blocks, BLOCK, HD)
    return turns


def early_kernel(count, capacity, seq_count, first, usable_ref, table, lower_ref, *rest):
    piece_refs = rest[:count]
    keys, values, count_ref = rest[count:]
    rows = piece_refs[0].shape[0] - FACTS
    group = Group(piece_refs, rows, capacity, seq_count, lower_ref, usable_ref, 0.0, first)
    spread_group(group, rows, table, keys, values, 0)
    count_ref[...] = group.count


def spread_early(usable, table, lower, pieces, first, capacity, seq_count, slots):
    vmem = pl.BlockSpec(memory_space=pltpu.VMEM)
    blocks = slots // BLOCK
    length = len(pieces) * BLOCK
    return pl.pallas_call(
        functools.partial(early_kernel, len(pieces), capacity, seq_count, first),
        in_specs=[pl.BlockSpec(memory_space=pltpu.SMEM)] + [vmem] * (2 + len(pieces)),
        out_shape=[
            jax.ShapeDtypeStruct((blocks, length, 2 * HD), bf16),
            jax.ShapeDtypeStruct((blocks, length, HD), bf16),
            jax.ShapeDtypeStruct((1, seq_count), f32),
        ],
        compiler_params=params(16),
        name="spread_early",
    )(usable, table, lower, *pieces)


def attention_kernel(count, capacity, seq_count, usable_ref, table, lower_ref, q_ref, *rest):
    early_keys, early_values, early_count, *rest = rest
    before_count = early_count[...]
    piece_refs = rest[:count]
    out_ref, keys, values, contexts, scores_ref, weights_ref = rest[count:]
    blocks = keys.shape[0]
    slots = blocks * BLOCK
    rows = q_ref.shape[0]
    group = Group(piece_refs, rows, capacity, seq_count, lower_ref, usable_ref, before_count, 0)
    own_turn = spread_group(group, rows, table, keys, values, 0)[:rows]
    queries = [turned(q_ref[:, h * HD : (h + 1) * HD].astype(f32), own_turn).astype(bf16) for h in range(HQ)]
    own_hot = one_hot(group.slots[0], slots)
    last = lax.broadcasted_iota(i32, (slots, HD), 1) == HD - 1
    q_slots = jnp.dot(own_hot, jnp.concatenate(queries, axis=1), preferred_element_type=f32).astype(bf16)
    q_marks = jnp.dot(own_hot, group.marks[0], preferred_element_type=f32)
    q_marks = (jnp.where(last, -1.0, q_marks - 1.0) * LARGE).astype(bf16)
    late = keys.shape[1]
    height = HQ * BLOCK
    contract = (((1,), (1,)), ((), ()))
    for block in range(blocks):
        at = slice(block * BLOCK, (block + 1) * BLOCK)
        q_block = q_slots[at, :]
        marks = q_marks[at, :]
        q_heads = jnp.concatenate(
            [jnp.concatenate([q_block[:, h * HD : (h + 1) * HD], marks], axis=1) for h in range(HQ)], axis=0
        )
        to = slice(block * height, (block + 1) * height)
        scores_ref[to, :late] = lax.dot_general(q_heads, keys[block], contract, preferred_element_type=f32)
        scores_ref[to, late:] = lax.dot_general(q_heads, early_keys[block], contract, preferred_element_type=f32)
    q_index = lax.broadcasted_iota(i32, (height, HD), 0) % BLOCK
    k_index = lax.broadcasted_iota(i32, (height, HD), 1)
    ordered = (k_index >= BLOCK) | (k_index <= q_index)
    rate = HD ** (-0.5)
    for block in range(blocks):
        to = slice(block * height, (block + 1) * height)
        scores = scores_ref[to, :]
        scores = jnp.concatenate([jnp.where(ordered, scores[:, :HD], -LARGE), scores[:, HD:]], axis=1)
        exponent = jnp.exp((scores - jnp.max(scores, axis=1, keepdims=True)) * rate)
        weights_ref[to, :] = (exponent * (1.0 / jnp.sum(exponent, axis=1, keepdims=True))).astype(bf16)
    for block in range(blocks):
        at = slice(block * BLOCK, (block + 1) * BLOCK)
        to = slice(block * height, (block + 1) * height)
        context = jnp.dot(weights_ref[to, :late], values[block], preferred_element_type=f32)
        context += jnp.dot(weights_ref[to, late:], early_values[block], preferred_element_type=f32)
        context = context.astype(bf16)
        for h in range(HQ):
            contexts[at, h * HD : (h + 1) * HD] = context[h * BLOCK : (h + 1) * BLOCK, :]
    out_ref[...] = lax.dot_general(
        own_hot, contexts[...], (((0,), (0,)), ((), ())), preferred_element_type=f32
    ).astype(bf16)


def attend(usable, table, lower, queries, early, pieces, capacity, seq_count, slots):
    rows = queries.shape[0]
    blocks = slots // BLOCK
    vmem = pl.BlockSpec(memory_space=pltpu.VMEM)
    count = len(pieces)
    late = count * BLOCK
    total = late + early[0].shape[1]
    height = blocks * HQ * BLOCK
    return pl.pallas_call(
        functools.partial(attention_kernel, count, capacity, seq_count),
        in_specs=[pl.BlockSpec(memory_space=pltpu.SMEM)] + [vmem] * (3 + len(early) + count),
        out_shape=jax.ShapeDtypeStruct((rows, QW), bf16),
        scratch_shapes=[
            pltpu.VMEM((blocks, late, 2 * HD), bf16),
            pltpu.VMEM((blocks, late, HD), bf16),
            pltpu.VMEM((slots, QW), bf16),
            pltpu.VMEM((height, total), f32),
            pltpu.VMEM((height, total), bf16),
        ],
        compiler_params=params(24),
        name="attention",
    )(usable, table, lower, queries, *early, *pieces)


def rotary(tensor, position):
    half_dim = tensor.shape[-1] // 2
    frequency = jnp.power(
        rope_base, -jnp.arange(half_dim, dtype=jnp.float32) * 2.0 / tensor.shape[-1]
    )
    rotation = position.astype(jnp.float32)[:, None] * frequency[None, :]
    cosine = jnp.cos(rotation)[:, None, :]
    sine_part = jnp.sin(rotation)[:, None, :]
    front_half = tensor[..., :half_dim]
    back_half = tensor[..., half_dim:]
    return jnp.concatenate(
        [front_half * cosine - back_half * sine_part, back_half * cosine + front_half * sine_part],
        axis=-1,
    )


def finish(query_sum, key_sum, value_sum, b_query, b_key, b_value):
    return jnp.concatenate(
        [
            (query_sum + b_query.astype(jnp.float32)).astype(jnp.bfloat16),
            (key_sum + b_key.astype(jnp.float32)).astype(jnp.bfloat16),
            (value_sum + b_value.astype(jnp.float32)).astype(jnp.bfloat16),
        ],
        axis=1,
    )


def project(source_rows, norm_gain, w_query, w_key, w_value, b_query, b_key, b_value):
    widened = source_rows.astype(jnp.float32)
    inverse = lax.rsqrt(jnp.mean(widened * widened, axis=1, keepdims=True) + epsilon)
    query_part = lax.all_gather(w_query, "fsdp", axis=0, tiled=True)
    key_part = lax.all_gather(w_key, "fsdp", axis=0, tiled=True)
    value_part = lax.all_gather(w_value, "fsdp", axis=0, tiled=True)
    gain_part = lax.all_gather(norm_gain, "fsdp", axis=0, tiled=True)
    normed_part = (
        source_rows.astype(jnp.float32) * inverse * gain_part.astype(jnp.float32)
    ).astype(jnp.bfloat16)
    query_sum = jnp.dot(normed_part, query_part, preferred_element_type=jnp.float32)
    key_sum = jnp.dot(normed_part, key_part, preferred_element_type=jnp.float32)
    value_sum = jnp.dot(normed_part, value_part, preferred_element_type=jnp.float32)
    return finish(query_sum, key_sum, value_sum, b_query, b_key, b_value)


def attend_at_host(projected, slot_ids):
    row_count = projected.shape[0]
    query_width = HQ * HD
    queries = projected[:, :query_width].reshape(row_count, HQ, HD)
    keys_raw = projected[:, query_width : query_width + HD]
    values_raw = projected[:, query_width + HD :]
    index_row = jnp.arange(row_count)
    same_slot = slot_ids[:, None] == slot_ids[None, :]
    position = jnp.sum(same_slot & (index_row[None, :] < index_row[:, None]), axis=1)
    allowed = same_slot & (index_row[None, :] <= index_row[:, None])
    query_rot = rotary(queries.astype(jnp.float32), position).astype(jnp.bfloat16)
    key_rot = rotary(keys_raw.astype(jnp.float32)[:, None, :], position)[:, 0, :].astype(
        jnp.bfloat16
    )
    scores = jnp.einsum(
        "qhd,kd->hqk", query_rot, key_rot, preferred_element_type=jnp.float32
    ) * HD ** (-0.5)
    scores = jnp.where(allowed[None, :, :], scores, -jnp.inf)
    largest = jnp.max(scores, axis=-1, keepdims=True)
    exponent = jnp.exp(scores - largest)
    attention = (exponent / jnp.sum(exponent, axis=-1, keepdims=True)).astype(jnp.bfloat16)
    context = jnp.einsum("hqk,kd->qhd", attention, values_raw, preferred_element_type=jnp.float32)
    return context.astype(jnp.bfloat16).reshape(row_count, query_width)


def per_device_exchanged(
    hidden, norm_gain, w_query, w_key, w_value, b_query, b_key, b_value, row_host, row_slot
):
    host_count = lax.axis_size(("dp", "fsdp"))
    source_count = hidden.shape[0]
    capacity = 2 * source_count // host_count
    index_row = jnp.arange(source_count)
    same_host = row_host[:, None] == row_host[None, :]
    row_rank = jnp.sum(same_host & (index_row[None, :] < index_row[:, None]), axis=1)
    slot_index = row_host * capacity + row_rank
    payload = project(hidden, norm_gain, w_query, w_key, w_value, b_query, b_key, b_value)
    payload_width = payload.shape[1]
    outgoing = (
        jnp.zeros((host_count * capacity, payload_width), jnp.bfloat16).at[slot_index].set(payload)
    )
    slot_out = jnp.full((host_count * capacity,), -1, jnp.int32).at[slot_index].set(row_slot)
    arrived, slot_ids = (
        lax.all_to_all(
            outgoing.reshape(host_count, capacity, payload_width),
            ("dp", "fsdp"),
            split_axis=0,
            concat_axis=0,
            tiled=True,
        ),
        lax.all_to_all(
            slot_out.reshape(host_count, capacity),
            ("dp", "fsdp"),
            split_axis=0,
            concat_axis=0,
            tiled=True,
        ),
    )
    arrived = arrived.reshape(host_count * capacity, payload_width)
    slot_ids = slot_ids.reshape(host_count * capacity)
    context = attend_at_host(arrived, slot_ids)
    returned = lax.all_to_all(
        context.reshape(host_count, capacity, context.shape[1]),
        ("dp", "fsdp"),
        split_axis=0,
        concat_axis=0,
        tiled=True,
    )
    return returned.reshape(host_count * capacity, context.shape[1])[slot_index]


def swap_cores(array):
    return lax.ppermute(array, "fsdp", [(0, 1), (1, 0)])


def far(array, shift):
    count = lax.axis_size("dp")
    return lax.ppermute(array, "dp", [(i, (i + shift * 2) % count) for i in range(count)])


def swap_near(array):
    count = lax.axis_size("dp")
    return lax.ppermute(array, "dp", [(i, i ^ 1) for i in range(count)])


def after(array, *others):
    return lax.optimization_barrier((array, *others))[0]


def per_device_stepped(
    hidden, norm_gain, w_query, w_key, w_value, b_query, b_key, b_value, row_host, row_slot
):
    host_count = lax.axis_size(("dp", "fsdp"))
    rows = hidden.shape[0]
    capacity = 2 * rows // host_count
    slots = host_count * capacity
    seq_count = host_count * SLOTS_PER_HOST
    row, core = lax.axis_index("dp"), lax.axis_index("fsdp")
    me = lax.axis_index(("dp", "fsdp"))
    index = jnp.arange(host_count)
    far_row = (row // 2 - index // 4) % 4
    sources = far_row * 4 + ((row % 2) ^ ((index // 2) % 2)) * 2 + (core ^ (index % 2))
    usable = (sources <= me).astype(i32)
    lower = ((sources[None, :] < sources[:, None]) & (usable[None, :] > 0)).astype(f32)
    table = jnp.asarray(rotary_table(2 * rows))
    which = core.reshape(1)

    gain_other = swap_cores(norm_gain)
    w_value_other = swap_cores(w_value)
    w_key_other = swap_cores(w_key)
    pairs, normed = keys_and_values(
        which, gain_other, hidden, w_key, w_value, w_key_other, w_value_other,
        norm_gain, b_key, b_value, row_host, row_slot,
    )
    w_query_other = swap_cores(after(w_query, w_key_other, w_value_other, gain_other))
    first_half = query_half(True, which, normed, w_query)
    lines = {0: pairs}
    for shift in (2, 3, 1):
        lines[shift] = far(after(pairs, first_half) if shift == 1 else pairs, shift)
    queries = query_half(False, which, normed, w_query_other, first_half, b_query)
    nears = [swap_near(lines[shift]) for shift in range(4)]
    early_pieces = []
    for shift in (2, 3):
        for here in (lines[shift], nears[shift]):
            early_pieces += [here, swap_cores(here)]
    early = spread_early(usable, table, lower, early_pieces, 8, capacity, seq_count, slots)
    late = []
    for shift in (0, 1):
        for here in (lines[shift], nears[shift]):
            sent = after(here, early[2], queries) if shift == 1 and here is nears[1] else here
            late += [here, swap_cores(sent)]
    return attend(usable, table, lower, queries, early, late, capacity, seq_count, slots)


def per_device(*args):
    if lax.axis_size("dp") == 8:
        return per_device_stepped(*args)
    return per_device_exchanged(*args)


def solution(mesh):
    return jax.shard_map(
        per_device,
        mesh=mesh,
        in_specs=(
            P(("groups", "dp", "fsdp"), None),
            P("fsdp"),
            P("fsdp", None),
            P("fsdp", None),
            P("fsdp", None),
            P(),
            P(),
            P(),
            P(("groups", "dp", "fsdp")),
            P(("groups", "dp", "fsdp")),
        ),
        out_specs=P(("groups", "dp", "fsdp"), None),
        check_vma=False,
    )
```

```python
import functools
import jax
import jax.numpy as jnp
import numpy as np
from jax import lax
from jax.experimental import pallas as pl
from jax.experimental.pallas import tpu as pltpu
from jax.sharding import PartitionSpec as P

HD = 128
HQ = 4
QW = HQ * HD
SLOTS_PER_HOST = 8
BLOCK = 32
LARGE = 1e30
FACTS = 16
KV_MIB = 56
rope_base = 1000000.0
epsilon = 1e-06
f32 = jnp.float32
bf16 = jnp.bfloat16
i32 = jnp.int32
MIB = 1024 * 1024
ANYWHERE = pl.BlockSpec(memory_space=pltpu.HBM)
FREE = pl.BlockSpec(memory_space=pl.ANY)


def params(mib=58):
    return pltpu.CompilerParams(vmem_limit_bytes=mib * MIB)


def whole(shape):
    return pl.BlockSpec(shape, lambda *i: (0,) * len(shape))


def rotary_table(positions):
    frequency = np.power(np.float32(rope_base), -np.arange(HD // 2, dtype=np.float32) * np.float32(2.0 / HD))
    rotation = np.arange(positions, dtype=np.float32)[:, None] * frequency.astype(np.float32)[None, :]
    rotation = rotation.astype(np.float64)
    rest = np.concatenate([np.cos(rotation), np.sin(rotation)], axis=1).astype(np.float32)
    terms = []
    for _ in range(2):
        term = rest.astype(jnp.bfloat16)
        terms.append(term)
        rest = rest - term.astype(np.float32)
    return np.concatenate(terms, axis=1)


def key_value_kernel(core_ref, hidden_hbm, *rest):
    weights_hbm, small_hbm, rest = rest[:4], rest[4:10], rest[10:]
    out_ref, normed_hbm, hidden, normed, gains, wk, wv, wk_other, wv_other, *rest = rest
    small, (in_sems, sems, out_sems) = rest[:6], rest[6:]
    gain_ref, gain_other_ref, bk_ref, bv_ref, host_ref, slot_ref = small
    rows, width = hidden.shape
    half = width // 2
    core = core_ref[0]
    own_at = pl.multiple_of(core * half, half)
    other_at = pl.multiple_of((1 - core) * half, half)
    parts = in_sems.shape[0]
    part_rows = rows // parts
    lanes = 1024
    high = 8

    small_copies = [pltpu.make_async_copy(a, b, sems.at[4 + i]) for i, (a, b) in enumerate(zip(small_hbm, small))]
    weights = (wk, wv, wk_other, wv_other)
    weight_copies = [pltpu.make_async_copy(a, b, sems.at[i]) for i, (a, b) in enumerate(zip(weights_hbm, weights))]

    def span(i):
        return pl.ds(i * part_rows, part_rows)

    loads = [pltpu.make_async_copy(hidden_hbm.at[span(i), :], hidden.at[span(i), :], in_sems.at[i]) for i in range(parts)]
    saves = [pltpu.make_async_copy(normed.at[span(i), :], normed_hbm.at[span(i), :], out_sems.at[i]) for i in range(parts)]
    for c in small_copies + loads + weight_copies:
        c.start()
    for c in small_copies:
        c.wait()
    gains[:, pl.ds(own_at, half)] = jnp.broadcast_to(gain_ref[...].astype(f32)[None, :], (high, half))
    gains[:, pl.ds(other_at, half)] = jnp.broadcast_to(gain_other_ref[...].astype(f32)[None, :], (high, half))
    tail = out_ref.shape[0] - rows
    line = lax.broadcasted_iota(i32, (tail, rows), 0)
    facts = jnp.where(line == 0, host_ref[...][None, :], jnp.where(line == 1, slot_ref[...][None, :], 0))
    out_ref[rows:, :] = facts.astype(f32).astype(bf16)

    for i in range(parts):
        at = slice(i * part_rows, (i + 1) * part_rows)
        loads[i].wait()
        total = jnp.zeros((part_rows, lanes), f32)
        for j in range(width // lanes):
            wide = hidden[at, j * lanes : (j + 1) * lanes].astype(f32)
            total += wide * wide
        mean = jnp.sum(total, axis=1, keepdims=True) * (1.0 / width)
        scale = lax.rsqrt(mean + epsilon)
        for j in range(width // lanes):
            to = slice(j * lanes, (j + 1) * lanes)
            wide = (hidden[at, to].astype(f32) * scale).reshape(part_rows // high, high, lanes)
            normed[at, to] = (wide * gains[:, to][None]).reshape(part_rows, lanes).astype(bf16)
        saves[i].start()
    for c in weight_copies[:2]:
        c.wait()
    total = jnp.dot(
        normed[:, pl.ds(own_at, half)], jnp.concatenate([wk[...], wv[...]], axis=1), preferred_element_type=f32
    )
    for c in weight_copies[2:]:
        c.wait()
    total += jnp.dot(
        normed[:, pl.ds(other_at, half)],
        jnp.concatenate([wk_other[...], wv_other[...]], axis=1),
        preferred_element_type=f32,
    )
    out_ref[:rows, :HD] = (total[:, :HD] + bk_ref[...].astype(f32)[None, :]).astype(bf16)
    out_ref[:rows, HD:] = (total[:, HD:] + bv_ref[...].astype(f32)[None, :]).astype(bf16)
    for c in saves:
        c.wait()


def keys_and_values(core, hidden, w_key, w_value, wk_other, wv_other, *small):
    rows, width = hidden.shape
    half = width // 2
    parts = 8
    vmem = pl.BlockSpec(memory_space=pltpu.VMEM)
    return pl.pallas_call(
        key_value_kernel,
        in_specs=[pl.BlockSpec(memory_space=pltpu.SMEM)] + [ANYWHERE] * 3 + [FREE] * (2 + len(small)),
        out_specs=[vmem, ANYWHERE],
        out_shape=[
            jax.ShapeDtypeStruct((rows + FACTS, 2 * HD), bf16),
            jax.ShapeDtypeStruct((rows, width), bf16),
        ],
        scratch_shapes=[
            pltpu.VMEM((rows, width), bf16),
            pltpu.VMEM((rows, width), bf16),
            pltpu.VMEM((8, width), f32),
            *[pltpu.VMEM((half, HD), bf16)] * 4,
            *[pltpu.VMEM(a.shape, a.dtype) for a in small],
            pltpu.SemaphoreType.DMA((parts,)),
            pltpu.SemaphoreType.DMA((4 + len(small),)),
            pltpu.SemaphoreType.DMA((parts,)),
        ],
        compiler_params=params(62),
        cost_estimate=pl.CostEstimate(flops=8 * rows * half * HD, bytes_accessed=10 * MIB, transcendentals=0),
        name="keys_values",
    )(core, hidden, w_key, w_value, wk_other, wv_other, *small)


def query_kernel(mine, core_ref, rows_hbm, weights_hbm, *rest):
    if mine:
        out_ref, rows, weights, sems = rest
    else:
        sum_hbm, b_hbm, out_ref, rows, weights, total_ref, b_ref, sems = rest
    half = weights.shape[0]
    parts = 4
    chunk = half // parts
    side = core_ref[0] if mine else 1 - core_ref[0]
    copies = []
    for i in range(parts):
        at = pl.ds(i * chunk, chunk)
        source = pl.ds(pl.multiple_of(side * half + i * chunk, chunk), chunk)
        copies.append(pltpu.make_async_copy(rows_hbm.at[:, source], rows.at[:, at], sems.at[2 * i]))
        copies.append(pltpu.make_async_copy(weights_hbm.at[at, :], weights.at[at, :], sems.at[2 * i + 1]))
    if not mine:
        copies.append(pltpu.make_async_copy(sum_hbm, total_ref, sems.at[2 * parts]))
        copies.append(pltpu.make_async_copy(b_hbm, b_ref, sems.at[2 * parts + 1]))
    for c in copies:
        c.start()
    total = None
    for i in range(parts):
        copies[2 * i].wait()
        copies[2 * i + 1].wait()
        at = slice(i * chunk, (i + 1) * chunk)
        here = jnp.dot(rows[:, at], weights[at, :], preferred_element_type=f32)
        total = here if total is None else total + here
    if mine:
        out_ref[...] = total
    else:
        copies[-2].wait()
        copies[-1].wait()
        out_ref[...] = (total + total_ref[...] + b_ref[...].astype(f32)[None, :]).astype(bf16)


def query_half(mine, core, normed, weights, *more):
    rows = normed.shape[0]
    half = weights.shape[0]
    extra = [] if mine else [pltpu.VMEM((rows, QW), f32), pltpu.VMEM((QW,), bf16)]
    return pl.pallas_call(
        functools.partial(query_kernel, mine),
        in_specs=[pl.BlockSpec(memory_space=pltpu.SMEM)] + [ANYWHERE] * (2 + len(more)),
        out_shape=jax.ShapeDtypeStruct((rows, QW), f32 if mine else bf16),
        scratch_shapes=[
            pltpu.VMEM((rows, half), bf16),
            pltpu.VMEM((half, QW), bf16),
            *extra,
            pltpu.SemaphoreType.DMA((10,)),
        ],
        compiler_params=params(KV_MIB),
        cost_estimate=pl.CostEstimate(flops=2 * rows * half * QW, bytes_accessed=6 * MIB, transcendentals=0),
        name="queries_own" if mine else "queries_other",
    )(core, normed, weights, *more)


class Group:
    def __init__(self, pieces, rows, capacity, seq_count, lower_ref, usable_ref, before_count, first):
        self.pieces = pieces
        count = len(pieces)
        shift = SLOTS_PER_HOST.bit_length() - 1
        facts = [p[rows:, :].astype(f32) for p in pieces]
        hosts = jnp.concatenate([f[0:1] for f in facts], axis=0).astype(i32)
        seqs = hosts * SLOTS_PER_HOST + jnp.concatenate([f[1:2] for f in facts], axis=0).astype(i32)
        padded = jnp.concatenate([seqs, jnp.zeros((HD - count, rows), i32)], axis=0)
        columns = jnp.transpose(padded.astype(f32)).astype(i32)
        at_row = lax.broadcasted_iota(i32, (rows, rows), 0)
        at_lane = lax.broadcasted_iota(i32, (rows, rows), 1)
        before = jnp.where(at_row < at_lane, 1, 0)
        below = jnp.where(at_lane < at_row, 1.0, 0.0).astype(bf16)
        seq_lanes = lax.broadcasted_iota(i32, (rows, seq_count), 1)
        code_lanes = lax.broadcasted_iota(i32, (rows, HD), 1)
        codes_in_block = SLOTS_PER_HOST * BLOCK // capacity
        hots, counts, self.slots, self.marks = [], [], [], []
        for p in range(count):
            column = columns[:, p : p + 1]
            hot = jnp.where(seq_lanes == column, 1.0, 0.0)
            hots.append(hot)
            counts.append(jnp.sum(hot, axis=0, keepdims=True))
            same = lax.shift_right_logical(column, shift) == hosts[p : p + 1, :]
            rank = jnp.sum(jnp.where(same, before, 0), axis=0, keepdims=True)
            self.slots.append(hosts[p : p + 1, :] * capacity + rank)
            code = jnp.where(usable_ref[first + p] > 0, lax.bitwise_and(column, codes_in_block - 1), -1)
            mark = (code_lanes == code) | ((code_lanes == HD - 1) & (code >= 0))
            self.marks.append(jnp.where(mark, 1.0, 0.0).astype(bf16))
        base = jnp.zeros((count, seq_count), f32) + before_count
        for q in range(count):
            base = base + lower_ref[first : first + count, first + q : first + q + 1] * counts[q]
        self.positions = []
        ranks = jnp.dot(below, jnp.concatenate(hots, axis=1).astype(bf16), preferred_element_type=f32)
        for p in range(count):
            earlier = ranks[:, p * seq_count : (p + 1) * seq_count] + base[p : p + 1, :]
            self.positions.append(jnp.sum(hots[p] * earlier, axis=1, keepdims=True).astype(i32))
        self.count = before_count
        for q in range(count):
            self.count = self.count + jnp.where(usable_ref[first + q] > 0, counts[q], 0.0)

    def turns(self, table):
        position = jnp.concatenate(self.positions, axis=0)
        places = lax.broadcasted_iota(i32, (position.shape[0], table.shape[0]), 1)
        hot = jnp.where(places == position, 1.0, 0.0).astype(bf16)
        terms = jnp.dot(hot, table[...], preferred_element_type=f32)
        return terms[:, :HD] + terms[:, HD:]


def turned(block, turn):
    half = HD // 2
    first = lax.broadcasted_iota(i32, block.shape, 1) < half
    other_turn = pltpu.roll(turn, half, 1)
    cosine = jnp.where(first, turn, other_turn)
    sine = jnp.where(first, -other_turn, turn)
    return block * cosine + pltpu.roll(block, half, 1) * sine


def one_hot(slot_row, slots):
    rows = slot_row.shape[1]
    at = lax.broadcasted_iota(i32, (slots, rows), 0)
    return jnp.where(at == slot_row, 1.0, 0.0).astype(bf16)


def spread_group(group, rows, table, keys, values, at_piece):
    blocks = keys.shape[0]
    slots = blocks * BLOCK
    last = lax.broadcasted_iota(i32, (slots, HD), 1) == HD - 1
    turns = group.turns(table)
    raw = jnp.concatenate([piece[:rows, :HD] for piece in group.pieces], axis=0)
    own_keys = turned(raw.astype(f32), turns).astype(bf16)
    for p, piece in enumerate(group.pieces):
        hot = one_hot(group.slots[p], slots)
        at = slice((at_piece + p) * BLOCK, (at_piece + p + 1) * BLOCK)
        both = jnp.concatenate([own_keys[p * rows : (p + 1) * rows], group.marks[p], piece[:rows, HD:]], axis=1)
        moved = jnp.dot(hot, both, preferred_element_type=f32)
        marks = moved[:, HD : 2 * HD]
        marks = jnp.where(last, 1.0 - marks, marks)
        keys[:, at, :HD] = moved[:, :HD].astype(bf16).reshape(blocks, BLOCK, HD)
        keys[:, at, HD:] = marks.astype(bf16).reshape(blocks, BLOCK, HD)
        values[:, at, :] = moved[:, 2 * HD :].astype(bf16).reshape(blocks, BLOCK, HD)
    return turns


def early_kernel(count, capacity, seq_count, first, usable_ref, table, lower_ref, *rest):
    piece_refs = rest[:count]
    keys, values, count_ref = rest[count:]
    rows = piece_refs[0].shape[0] - FACTS
    group = Group(piece_refs, rows, capacity, seq_count, lower_ref, usable_ref, 0.0, first)
    spread_group(group, rows, table, keys, values, 0)
    count_ref[...] = group.count


def spread_early(usable, table, lower, pieces, first, capacity, seq_count, slots):
    vmem = pl.BlockSpec(memory_space=pltpu.VMEM)
    blocks = slots // BLOCK
    length = len(pieces) * BLOCK
    return pl.pallas_call(
        functools.partial(early_kernel, len(pieces), capacity, seq_count, first),
        in_specs=[pl.BlockSpec(memory_space=pltpu.SMEM)] + [vmem] * (2 + len(pieces)),
        out_shape=[
            jax.ShapeDtypeStruct((blocks, length, 2 * HD), bf16),
            jax.ShapeDtypeStruct((blocks, length, HD), bf16),
            jax.ShapeDtypeStruct((1, seq_count), f32),
        ],
        compiler_params=params(16),
        name="spread_early",
    )(usable, table, lower, *pieces)


def attention_kernel(count, capacity, seq_count, usable_ref, table, lower_ref, q_hbm, *rest):
    early_keys, early_values, early_count, *rest = rest
    before_count = early_count[...]
    piece_refs = rest[:count]
    out_ref, keys, values, contexts, scores_ref, weights_ref, q_ref, q_sem = rest[count:]
    load = pltpu.make_async_copy(q_hbm, q_ref, q_sem)
    load.start()
    blocks = keys.shape[0]
    slots = blocks * BLOCK
    rows = q_ref.shape[0]
    group = Group(piece_refs, rows, capacity, seq_count, lower_ref, usable_ref, before_count, 0)
    own_turn = spread_group(group, rows, table, keys, values, 0)[:rows]
    load.wait()
    queries = [turned(q_ref[:, h * HD : (h + 1) * HD].astype(f32), own_turn).astype(bf16) for h in range(HQ)]
    own_hot = one_hot(group.slots[0], slots)
    last = lax.broadcasted_iota(i32, (slots, HD), 1) == HD - 1
    q_slots = jnp.dot(own_hot, jnp.concatenate(queries, axis=1), preferred_element_type=f32).astype(bf16)
    q_marks = jnp.dot(own_hot, group.marks[0], preferred_element_type=f32)
    q_marks = (jnp.where(last, -1.0, q_marks - 1.0) * LARGE).astype(bf16)
    late = keys.shape[1]
    height = HQ * BLOCK
    contract = (((1,), (1,)), ((), ()))
    for block in range(blocks):
        at = slice(block * BLOCK, (block + 1) * BLOCK)
        q_block = q_slots[at, :]
        marks = q_marks[at, :]
        q_heads = jnp.concatenate(
            [jnp.concatenate([q_block[:, h * HD : (h + 1) * HD], marks], axis=1) for h in range(HQ)], axis=0
        )
        to = slice(block * height, (block + 1) * height)
        scores_ref[to, :late] = lax.dot_general(q_heads, keys[block], contract, preferred_element_type=f32)
        scores_ref[to, late:] = lax.dot_general(q_heads, early_keys[block], contract, preferred_element_type=f32)
    q_index = lax.broadcasted_iota(i32, (height, HD), 0) % BLOCK
    k_index = lax.broadcasted_iota(i32, (height, HD), 1)
    ordered = (k_index >= BLOCK) | (k_index <= q_index)
    rate = HD ** (-0.5)
    for block in range(blocks):
        to = slice(block * height, (block + 1) * height)
        scores = scores_ref[to, :]
        scores = jnp.concatenate([jnp.where(ordered, scores[:, :HD], -LARGE), scores[:, HD:]], axis=1)
        exponent = jnp.exp((scores - jnp.max(scores, axis=1, keepdims=True)) * rate)
        weights_ref[to, :] = (exponent * (1.0 / jnp.sum(exponent, axis=1, keepdims=True))).astype(bf16)
    for block in range(blocks):
        at = slice(block * BLOCK, (block + 1) * BLOCK)
        to = slice(block * height, (block + 1) * height)
        context = jnp.dot(weights_ref[to, :late], values[block], preferred_element_type=f32)
        context += jnp.dot(weights_ref[to, late:], early_values[block], preferred_element_type=f32)
        context = context.astype(bf16)
        for h in range(HQ):
            contexts[at, h * HD : (h + 1) * HD] = context[h * BLOCK : (h + 1) * BLOCK, :]
    out_ref[...] = lax.dot_general(
        own_hot, contexts[...], (((0,), (0,)), ((), ())), preferred_element_type=f32
    ).astype(bf16)


def attend(usable, table, lower, queries, early, pieces, capacity, seq_count, slots):
    rows = queries.shape[0]
    blocks = slots // BLOCK
    vmem = pl.BlockSpec(memory_space=pltpu.VMEM)
    count = len(pieces)
    late = count * BLOCK
    total = late + early[0].shape[1]
    height = blocks * HQ * BLOCK
    return pl.pallas_call(
        functools.partial(attention_kernel, count, capacity, seq_count),
        in_specs=[pl.BlockSpec(memory_space=pltpu.SMEM), vmem, vmem, FREE] + [vmem] * (len(early) + count),
        out_shape=jax.ShapeDtypeStruct((rows, QW), bf16),
        scratch_shapes=[
            pltpu.VMEM((blocks, late, 2 * HD), bf16),
            pltpu.VMEM((blocks, late, HD), bf16),
            pltpu.VMEM((slots, QW), bf16),
            pltpu.VMEM((height, total), f32),
            pltpu.VMEM((height, total), bf16),
            pltpu.VMEM((rows, QW), bf16),
            pltpu.SemaphoreType.DMA,
        ],
        compiler_params=params(24),
        name="attention",
    )(usable, table, lower, queries, *early, *pieces)


def rotary(tensor, position):
    half_dim = tensor.shape[-1] // 2
    frequency = jnp.power(
        rope_base, -jnp.arange(half_dim, dtype=jnp.float32) * 2.0 / tensor.shape[-1]
    )
    rotation = position.astype(jnp.float32)[:, None] * frequency[None, :]
    cosine = jnp.cos(rotation)[:, None, :]
    sine_part = jnp.sin(rotation)[:, None, :]
    front_half = tensor[..., :half_dim]
    back_half = tensor[..., half_dim:]
    return jnp.concatenate(
        [front_half * cosine - back_half * sine_part, back_half * cosine + front_half * sine_part],
        axis=-1,
    )


def finish(query_sum, key_sum, value_sum, b_query, b_key, b_value):
    return jnp.concatenate(
        [
            (query_sum + b_query.astype(jnp.float32)).astype(jnp.bfloat16),
            (key_sum + b_key.astype(jnp.float32)).astype(jnp.bfloat16),
            (value_sum + b_value.astype(jnp.float32)).astype(jnp.bfloat16),
        ],
        axis=1,
    )


def project(source_rows, norm_gain, w_query, w_key, w_value, b_query, b_key, b_value):
    widened = source_rows.astype(jnp.float32)
    inverse = lax.rsqrt(jnp.mean(widened * widened, axis=1, keepdims=True) + epsilon)
    query_part = lax.all_gather(w_query, "fsdp", axis=0, tiled=True)
    key_part = lax.all_gather(w_key, "fsdp", axis=0, tiled=True)
    value_part = lax.all_gather(w_value, "fsdp", axis=0, tiled=True)
    gain_part = lax.all_gather(norm_gain, "fsdp", axis=0, tiled=True)
    normed_part = (
        source_rows.astype(jnp.float32) * inverse * gain_part.astype(jnp.float32)
    ).astype(jnp.bfloat16)
    query_sum = jnp.dot(normed_part, query_part, preferred_element_type=jnp.float32)
    key_sum = jnp.dot(normed_part, key_part, preferred_element_type=jnp.float32)
    value_sum = jnp.dot(normed_part, value_part, preferred_element_type=jnp.float32)
    return finish(query_sum, key_sum, value_sum, b_query, b_key, b_value)


def attend_at_host(projected, slot_ids):
    row_count = projected.shape[0]
    query_width = HQ * HD
    queries = projected[:, :query_width].reshape(row_count, HQ, HD)
    keys_raw = projected[:, query_width : query_width + HD]
    values_raw = projected[:, query_width + HD :]
    index_row = jnp.arange(row_count)
    same_slot = slot_ids[:, None] == slot_ids[None, :]
    position = jnp.sum(same_slot & (index_row[None, :] < index_row[:, None]), axis=1)
    allowed = same_slot & (index_row[None, :] <= index_row[:, None])
    query_rot = rotary(queries.astype(jnp.float32), position).astype(jnp.bfloat16)
    key_rot = rotary(keys_raw.astype(jnp.float32)[:, None, :], position)[:, 0, :].astype(
        jnp.bfloat16
    )
    scores = jnp.einsum(
        "qhd,kd->hqk", query_rot, key_rot, preferred_element_type=jnp.float32
    ) * HD ** (-0.5)
    scores = jnp.where(allowed[None, :, :], scores, -jnp.inf)
    largest = jnp.max(scores, axis=-1, keepdims=True)
    exponent = jnp.exp(scores - largest)
    attention = (exponent / jnp.sum(exponent, axis=-1, keepdims=True)).astype(jnp.bfloat16)
    context = jnp.einsum("hqk,kd->qhd", attention, values_raw, preferred_element_type=jnp.float32)
    return context.astype(jnp.bfloat16).reshape(row_count, query_width)


def per_device_exchanged(
    hidden, norm_gain, w_query, w_key, w_value, b_query, b_key, b_value, row_host, row_slot
):
    host_count = lax.axis_size(("dp", "fsdp"))
    source_count = hidden.shape[0]
    capacity = 2 * source_count // host_count
    index_row = jnp.arange(source_count)
    same_host = row_host[:, None] == row_host[None, :]
    row_rank = jnp.sum(same_host & (index_row[None, :] < index_row[:, None]), axis=1)
    slot_index = row_host * capacity + row_rank
    payload = project(hidden, norm_gain, w_query, w_key, w_value, b_query, b_key, b_value)
    payload_width = payload.shape[1]
    outgoing = (
        jnp.zeros((host_count * capacity, payload_width), jnp.bfloat16).at[slot_index].set(payload)
    )
    slot_out = jnp.full((host_count * capacity,), -1, jnp.int32).at[slot_index].set(row_slot)
    arrived, slot_ids = (
        lax.all_to_all(
            outgoing.reshape(host_count, capacity, payload_width),
            ("dp", "fsdp"),
            split_axis=0,
            concat_axis=0,
            tiled=True,
        ),
        lax.all_to_all(
            slot_out.reshape(host_count, capacity),
            ("dp", "fsdp"),
            split_axis=0,
            concat_axis=0,
            tiled=True,
        ),
    )
    arrived = arrived.reshape(host_count * capacity, payload_width)
    slot_ids = slot_ids.reshape(host_count * capacity)
    context = attend_at_host(arrived, slot_ids)
    returned = lax.all_to_all(
        context.reshape(host_count, capacity, context.shape[1]),
        ("dp", "fsdp"),
        split_axis=0,
        concat_axis=0,
        tiled=True,
    )
    return returned.reshape(host_count * capacity, context.shape[1])[slot_index]


def swap_cores(array):
    return lax.ppermute(array, "fsdp", [(0, 1), (1, 0)])


def far(array, shift):
    count = lax.axis_size("dp")
    return lax.ppermute(array, "dp", [(i, (i + shift * 2) % count) for i in range(count)])


def swap_near(array):
    count = lax.axis_size("dp")
    return lax.ppermute(array, "dp", [(i, i ^ 1) for i in range(count)])


def after(array, *others):
    return lax.optimization_barrier((array, *others))[0]


def per_device_stepped(
    hidden, norm_gain, w_query, w_key, w_value, b_query, b_key, b_value, row_host, row_slot
):
    host_count = lax.axis_size(("dp", "fsdp"))
    rows = hidden.shape[0]
    capacity = 2 * rows // host_count
    slots = host_count * capacity
    seq_count = host_count * SLOTS_PER_HOST
    row, core = lax.axis_index("dp"), lax.axis_index("fsdp")
    me = lax.axis_index(("dp", "fsdp"))
    index = jnp.arange(host_count)
    far_row = (row // 2 - index // 4) % 4
    sources = far_row * 4 + ((row % 2) ^ ((index // 2) % 2)) * 2 + (core ^ (index % 2))
    usable = (sources <= me).astype(i32)
    lower = ((sources[None, :] < sources[:, None]) & (usable[None, :] > 0)).astype(f32)
    table = jnp.asarray(rotary_table(2 * rows))
    which = core.reshape(1)

    gain_other = swap_cores(norm_gain)
    w_value_other = swap_cores(w_value)
    w_key_other = swap_cores(w_key)
    pairs, normed = keys_and_values(
        which, hidden, w_key, w_value, w_key_other, w_value_other,
        norm_gain, gain_other, b_key, b_value, row_host, row_slot,
    )
    w_query_other = swap_cores(after(w_query, w_key_other, w_value_other, gain_other))
    first_half = query_half(True, which, normed, w_query)
    lines = {0: pairs}
    for shift in (2, 3, 1):
        lines[shift] = far(pairs, shift)
    queries = query_half(False, which, normed, w_query_other, first_half, b_query)
    nears = [swap_near(after(lines[shift], queries) if shift in (1, 2) else lines[shift]) for shift in range(4)]
    early_pieces = []
    for shift in (2, 3):
        for here in (lines[shift], nears[shift]):
            early_pieces += [here, swap_cores(here)]
    early = spread_early(usable, table, lower, early_pieces, 8, capacity, seq_count, slots)
    late = []
    for shift in (0, 1):
        for here in (lines[shift], nears[shift]):
            sent = after(here, early[2]) if shift == 1 and here is nears[1] else here
            late += [here, swap_cores(sent)]
    return attend(usable, table, lower, queries, early, late, capacity, seq_count, slots)


def per_device(*args):
    if lax.axis_size("dp") == 8:
        return per_device_stepped(*args)
    return per_device_exchanged(*args)


def solution(mesh):
    return jax.shard_map(
        per_device,
        mesh=mesh,
        in_specs=(
            P(("groups", "dp", "fsdp"), None),
            P("fsdp"),
            P("fsdp", None),
            P("fsdp", None),
            P("fsdp", None),
            P(),
            P(),
            P(),
            P(("groups", "dp", "fsdp")),
            P(("groups", "dp", "fsdp")),
        ),
        out_specs=P(("groups", "dp", "fsdp"), None),
        check_vma=False,
    )
```

```python
import functools
import jax
import jax.numpy as jnp
import numpy as np
from jax import lax
from jax.experimental import pallas as pl
from jax.experimental.pallas import tpu as pltpu
from jax.sharding import PartitionSpec as P

HD = 128
HQ = 4
QW = HQ * HD
SLOTS_PER_HOST = 8
BLOCK = 32
LARGE = 1e30
FACTS = 16
KV_MIB = 56
rope_base = 1000000.0
epsilon = 1e-06
f32 = jnp.float32
bf16 = jnp.bfloat16
i32 = jnp.int32
MIB = 1024 * 1024
ANYWHERE = pl.BlockSpec(memory_space=pltpu.HBM)
FREE = pl.BlockSpec(memory_space=pl.ANY)


def params(mib=58):
    return pltpu.CompilerParams(vmem_limit_bytes=mib * MIB)


def whole(shape):
    return pl.BlockSpec(shape, lambda *i: (0,) * len(shape))


def rotary_table(positions):
    frequency = np.power(np.float32(rope_base), -np.arange(HD // 2, dtype=np.float32) * np.float32(2.0 / HD))
    rotation = np.arange(positions, dtype=np.float32)[:, None] * frequency.astype(np.float32)[None, :]
    rotation = rotation.astype(np.float64)
    rest = np.concatenate([np.cos(rotation), np.sin(rotation)], axis=1).astype(np.float32)
    terms = []
    for _ in range(2):
        term = rest.astype(jnp.bfloat16)
        terms.append(term)
        rest = rest - term.astype(np.float32)
    return np.concatenate(terms, axis=1)


def facts_kernel(host_ref, slot_ref, out_ref):
    host = host_ref[...][None, :]
    rows = host.shape[1]
    at_row = lax.broadcasted_iota(i32, (rows, rows), 0)
    at_lane = lax.broadcasted_iota(i32, (rows, rows), 1)
    column = jnp.sum(jnp.where(at_row == at_lane, host, 0), axis=1, keepdims=True)
    before = at_row < at_lane
    same_host = (column == host) & before
    rank = jnp.sum(jnp.where(same_host, 1, 0), axis=0, keepdims=True)
    line = lax.broadcasted_iota(i32, out_ref.shape, 0)
    facts = jnp.where(line == 0, host, jnp.where(line == 1, slot_ref[...][None, :], 0))
    facts = jnp.where(line == 2, rank, facts)
    out_ref[...] = facts.astype(f32).astype(bf16)


def facts_of(row_host, row_slot):
    vmem = pl.BlockSpec(memory_space=pltpu.VMEM)
    return pl.pallas_call(
        facts_kernel,
        in_specs=[vmem, vmem],
        out_shape=jax.ShapeDtypeStruct((FACTS, row_host.shape[0]), bf16),
        compiler_params=params(8),
        name="facts",
    )(row_host, row_slot)


def key_value_kernel(core_ref, hidden_hbm, *rest):
    weights_hbm, small_hbm, rest = rest[:4], rest[4:9], rest[9:]
    out_ref, normed_hbm, hidden, normed, gains, wk, wv, wk_other, wv_other, *rest = rest
    small, (in_sems, sems, out_sems) = rest[:5], rest[5:]
    gain_ref, gain_other_ref, bk_ref, bv_ref, facts_ref = small
    rows, width = hidden.shape
    half = width // 2
    core = core_ref[0]
    own_at = pl.multiple_of(core * half, half)
    other_at = pl.multiple_of((1 - core) * half, half)
    parts = in_sems.shape[0]
    part_rows = rows // parts
    lanes = 1024
    high = 8

    small_copies = [pltpu.make_async_copy(a, b, sems.at[4 + i]) for i, (a, b) in enumerate(zip(small_hbm, small))]
    weights = (wk, wv, wk_other, wv_other)
    weight_copies = [pltpu.make_async_copy(a, b, sems.at[i]) for i, (a, b) in enumerate(zip(weights_hbm, weights))]

    def span(i):
        return pl.ds(i * part_rows, part_rows)

    loads = [pltpu.make_async_copy(hidden_hbm.at[span(i), :], hidden.at[span(i), :], in_sems.at[i]) for i in range(parts)]
    saves = [pltpu.make_async_copy(normed.at[span(i), :], normed_hbm.at[span(i), :], out_sems.at[i]) for i in range(parts)]
    for c in small_copies + loads + weight_copies:
        c.start()
    for c in small_copies:
        c.wait()
    gains[:, pl.ds(own_at, half)] = jnp.broadcast_to(gain_ref[...].astype(f32)[None, :], (high, half))
    gains[:, pl.ds(other_at, half)] = jnp.broadcast_to(gain_other_ref[...].astype(f32)[None, :], (high, half))
    out_ref[rows:, :] = facts_ref[...]

    for i in range(parts):
        at = slice(i * part_rows, (i + 1) * part_rows)
        loads[i].wait()
        total = jnp.zeros((part_rows, lanes), f32)
        for j in range(width // lanes):
            wide = hidden[at, j * lanes : (j + 1) * lanes].astype(f32)
            total += wide * wide
        mean = jnp.sum(total, axis=1, keepdims=True) * (1.0 / width)
        scale = lax.rsqrt(mean + epsilon)
        for j in range(width // lanes):
            to = slice(j * lanes, (j + 1) * lanes)
            wide = (hidden[at, to].astype(f32) * scale).reshape(part_rows // high, high, lanes)
            normed[at, to] = (wide * gains[:, to][None]).reshape(part_rows, lanes).astype(bf16)
        saves[i].start()
    for c in weight_copies[:2]:
        c.wait()
    total = jnp.dot(
        normed[:, pl.ds(own_at, half)], jnp.concatenate([wk[...], wv[...]], axis=1), preferred_element_type=f32
    )
    for c in weight_copies[2:]:
        c.wait()
    total += jnp.dot(
        normed[:, pl.ds(other_at, half)],
        jnp.concatenate([wk_other[...], wv_other[...]], axis=1),
        preferred_element_type=f32,
    )
    out_ref[:rows, :HD] = (total[:, :HD] + bk_ref[...].astype(f32)[None, :]).astype(bf16)
    out_ref[:rows, HD:] = (total[:, HD:] + bv_ref[...].astype(f32)[None, :]).astype(bf16)
    for c in saves:
        c.wait()


def keys_and_values(core, hidden, w_key, w_value, wk_other, wv_other, *small):
    rows, width = hidden.shape
    half = width // 2
    parts = 8
    vmem = pl.BlockSpec(memory_space=pltpu.VMEM)
    return pl.pallas_call(
        key_value_kernel,
        in_specs=[pl.BlockSpec(memory_space=pltpu.SMEM)] + [ANYWHERE] * 3 + [FREE] * (2 + len(small)),
        out_specs=[vmem, ANYWHERE],
        out_shape=[
            jax.ShapeDtypeStruct((rows + FACTS, 2 * HD), bf16),
            jax.ShapeDtypeStruct((rows, width), bf16),
        ],
        scratch_shapes=[
            pltpu.VMEM((rows, width), bf16),
            pltpu.VMEM((rows, width), bf16),
            pltpu.VMEM((8, width), f32),
            *[pltpu.VMEM((half, HD), bf16)] * 4,
            *[pltpu.VMEM(a.shape, a.dtype) for a in small],
            pltpu.SemaphoreType.DMA((parts,)),
            pltpu.SemaphoreType.DMA((4 + len(small),)),
            pltpu.SemaphoreType.DMA((parts,)),
        ],
        compiler_params=params(62),
        cost_estimate=pl.CostEstimate(flops=8 * rows * half * HD, bytes_accessed=10 * MIB, transcendentals=0),
        name="keys_values",
    )(core, hidden, w_key, w_value, wk_other, wv_other, *small)


def query_kernel(mine, core_ref, rows_hbm, weights_hbm, *rest):
    if mine:
        out_ref, rows, weights, sems = rest
    else:
        sum_hbm, b_hbm, out_ref, rows, weights, total_ref, b_ref, sems = rest
    half = weights.shape[0]
    parts = 4
    chunk = half // parts
    side = core_ref[0] if mine else 1 - core_ref[0]
    copies = []
    for i in range(parts):
        at = pl.ds(i * chunk, chunk)
        source = pl.ds(pl.multiple_of(side * half + i * chunk, chunk), chunk)
        copies.append(pltpu.make_async_copy(rows_hbm.at[:, source], rows.at[:, at], sems.at[2 * i]))
        copies.append(pltpu.make_async_copy(weights_hbm.at[at, :], weights.at[at, :], sems.at[2 * i + 1]))
    if not mine:
        copies.append(pltpu.make_async_copy(sum_hbm, total_ref, sems.at[2 * parts]))
        copies.append(pltpu.make_async_copy(b_hbm, b_ref, sems.at[2 * parts + 1]))
    for c in copies:
        c.start()
    total = None
    for i in range(parts):
        copies[2 * i].wait()
        copies[2 * i + 1].wait()
        at = slice(i * chunk, (i + 1) * chunk)
        here = jnp.dot(rows[:, at], weights[at, :], preferred_element_type=f32)
        total = here if total is None else total + here
    if mine:
        out_ref[...] = total
    else:
        copies[-2].wait()
        copies[-1].wait()
        out_ref[...] = (total + total_ref[...] + b_ref[...].astype(f32)[None, :]).astype(bf16)


def query_half(mine, core, normed, weights, *more):
    rows = normed.shape[0]
    half = weights.shape[0]
    extra = [] if mine else [pltpu.VMEM((rows, QW), f32), pltpu.VMEM((QW,), bf16)]
    return pl.pallas_call(
        functools.partial(query_kernel, mine),
        in_specs=[pl.BlockSpec(memory_space=pltpu.SMEM)] + [ANYWHERE] * (2 + len(more)),
        out_shape=jax.ShapeDtypeStruct((rows, QW), f32 if mine else bf16),
        scratch_shapes=[
            pltpu.VMEM((rows, half), bf16),
            pltpu.VMEM((half, QW), bf16),
            *extra,
            pltpu.SemaphoreType.DMA((10,)),
        ],
        compiler_params=params(KV_MIB),
        cost_estimate=pl.CostEstimate(flops=2 * rows * half * QW, bytes_accessed=6 * MIB, transcendentals=0),
        name="queries_own" if mine else "queries_other",
    )(core, normed, weights, *more)


class Group:
    def __init__(self, pieces, rows, capacity, seq_count, lower_ref, usable_ref, before_count, first):
        self.pieces = pieces
        count = len(pieces)
        facts = [p[rows:, :].astype(f32) for p in pieces]
        hosts = jnp.concatenate([f[0:1] for f in facts], axis=0).astype(i32)
        seqs = hosts * SLOTS_PER_HOST + jnp.concatenate([f[1:2] for f in facts], axis=0).astype(i32)
        host_ranks = jnp.concatenate([f[2:3] for f in facts], axis=0).astype(i32)
        padded = jnp.concatenate([seqs, jnp.zeros((HD - count, rows), i32)], axis=0)
        columns = jnp.transpose(padded.astype(f32)).astype(i32)
        at_row = lax.broadcasted_iota(i32, (rows, rows), 0)
        at_lane = lax.broadcasted_iota(i32, (rows, rows), 1)
        below = jnp.where(at_lane < at_row, 1.0, 0.0).astype(bf16)
        seq_lanes = lax.broadcasted_iota(i32, (rows, seq_count), 1)
        code_lanes = lax.broadcasted_iota(i32, (rows, HD), 1)
        codes_in_block = SLOTS_PER_HOST * BLOCK // capacity
        hots, counts, self.slots, self.marks = [], [], [], []
        for p in range(count):
            column = jnp.broadcast_to(columns[:, p : p + 1], (rows, HD))
            hot = jnp.where(seq_lanes == column, 1.0, 0.0)
            hots.append(hot)
            counts.append(jnp.sum(hot, axis=0, keepdims=True))
            self.slots.append(hosts[p : p + 1, :] * capacity + host_ranks[p : p + 1, :])
            mark = (code_lanes == lax.bitwise_and(column, codes_in_block - 1)) | (code_lanes == HD - 1)
            here = jnp.where(usable_ref[first + p] > 0, 1.0, 0.0)
            self.marks.append(jnp.where(mark, here, 0.0).astype(bf16))
        base = jnp.zeros((count, seq_count), f32) + before_count
        for q in range(count):
            base = base + lower_ref[first : first + count, first + q : first + q + 1] * counts[q]
        self.positions = []
        ranks = jnp.dot(below, jnp.concatenate(hots, axis=1).astype(bf16), preferred_element_type=f32)
        for p in range(count):
            earlier = ranks[:, p * seq_count : (p + 1) * seq_count] + base[p : p + 1, :]
            self.positions.append(jnp.sum(hots[p] * earlier, axis=1, keepdims=True).astype(i32))
        self.count = before_count
        for q in range(count):
            self.count = self.count + jnp.where(usable_ref[first + q] > 0, counts[q], 0.0)

    def turns(self, table):
        position = jnp.concatenate(self.positions, axis=0)
        places = lax.broadcasted_iota(i32, (position.shape[0], table.shape[0]), 1)
        hot = jnp.where(places == position, 1.0, 0.0).astype(bf16)
        terms = jnp.dot(hot, table[...], preferred_element_type=f32)
        return terms[:, :HD] + terms[:, HD:]


def turned(block, turn):
    half = HD // 2
    first = lax.broadcasted_iota(i32, block.shape, 1) < half
    other_turn = pltpu.roll(turn, half, 1)
    cosine = jnp.where(first, turn, other_turn)
    sine = jnp.where(first, -other_turn, turn)
    return block * cosine + pltpu.roll(block, half, 1) * sine


def one_hot(slot_row, slots):
    rows = slot_row.shape[1]
    at = lax.broadcasted_iota(i32, (slots, rows), 0)
    return jnp.where(at == slot_row, 1.0, 0.0).astype(bf16)


def spread_group(group, rows, table, keys, values, at_piece):
    blocks = keys.shape[0]
    slots = blocks * BLOCK
    last = lax.broadcasted_iota(i32, (slots, HD), 1) == HD - 1
    turns = group.turns(table)
    raw = jnp.concatenate([piece[:rows, :HD] for piece in group.pieces], axis=0)
    own_keys = turned(raw.astype(f32), turns).astype(bf16)
    for p, piece in enumerate(group.pieces):
        hot = one_hot(group.slots[p], slots)
        at = slice((at_piece + p) * BLOCK, (at_piece + p + 1) * BLOCK)
        both = jnp.concatenate([own_keys[p * rows : (p + 1) * rows], group.marks[p], piece[:rows, HD:]], axis=1)
        moved = jnp.dot(hot, both, preferred_element_type=f32)
        marks = moved[:, HD : 2 * HD]
        marks = jnp.where(last, 1.0 - marks, marks)
        keys[:, at, :HD] = moved[:, :HD].astype(bf16).reshape(blocks, BLOCK, HD)
        keys[:, at, HD:] = marks.astype(bf16).reshape(blocks, BLOCK, HD)
        values[:, at, :] = moved[:, 2 * HD :].astype(bf16).reshape(blocks, BLOCK, HD)
    return turns


def early_kernel(count, capacity, seq_count, first, usable_ref, table, lower_ref, *rest):
    piece_refs = rest[:count]
    keys, values, count_ref = rest[count:]
    rows = piece_refs[0].shape[0] - FACTS
    group = Group(piece_refs, rows, capacity, seq_count, lower_ref, usable_ref, 0.0, first)
    spread_group(group, rows, table, keys, values, 0)
    count_ref[...] = group.count


def spread_early(usable, table, lower, pieces, first, capacity, seq_count, slots):
    vmem = pl.BlockSpec(memory_space=pltpu.VMEM)
    blocks = slots // BLOCK
    length = len(pieces) * BLOCK
    return pl.pallas_call(
        functools.partial(early_kernel, len(pieces), capacity, seq_count, first),
        in_specs=[pl.BlockSpec(memory_space=pltpu.SMEM)] + [vmem] * (2 + len(pieces)),
        out_shape=[
            jax.ShapeDtypeStruct((blocks, length, 2 * HD), bf16),
            jax.ShapeDtypeStruct((blocks, length, HD), bf16),
            jax.ShapeDtypeStruct((1, seq_count), f32),
        ],
        compiler_params=params(16),
        name="spread_early",
    )(usable, table, lower, *pieces)


def attention_kernel(count, capacity, seq_count, usable_ref, table, lower_ref, q_hbm, *rest):
    early_keys, early_values, early_count, *rest = rest
    before_count = early_count[...]
    piece_refs = rest[:count]
    out_ref, keys, values, contexts, scores_ref, weights_ref, q_ref, q_sem = rest[count:]
    load = pltpu.make_async_copy(q_hbm, q_ref, q_sem)
    load.start()
    blocks = keys.shape[0]
    slots = blocks * BLOCK
    rows = q_ref.shape[0]
    group = Group(piece_refs, rows, capacity, seq_count, lower_ref, usable_ref, before_count, 0)
    own_turn = spread_group(group, rows, table, keys, values, 0)[:rows]
    load.wait()
    queries = [turned(q_ref[:, h * HD : (h + 1) * HD].astype(f32), own_turn).astype(bf16) for h in range(HQ)]
    own_hot = one_hot(group.slots[0], slots)
    last = lax.broadcasted_iota(i32, (slots, HD), 1) == HD - 1
    q_slots = jnp.dot(own_hot, jnp.concatenate(queries, axis=1), preferred_element_type=f32).astype(bf16)
    q_marks = jnp.dot(own_hot, group.marks[0], preferred_element_type=f32)
    q_marks = (jnp.where(last, -1.0, q_marks - 1.0) * LARGE).astype(bf16)
    late = keys.shape[1]
    height = HQ * BLOCK
    contract = (((1,), (1,)), ((), ()))
    for block in range(blocks):
        at = slice(block * BLOCK, (block + 1) * BLOCK)
        q_block = q_slots[at, :]
        marks = q_marks[at, :]
        q_heads = jnp.concatenate(
            [jnp.concatenate([q_block[:, h * HD : (h + 1) * HD], marks], axis=1) for h in range(HQ)], axis=0
        )
        to = slice(block * height, (block + 1) * height)
        scores_ref[to, :late] = lax.dot_general(q_heads, keys[block], contract, preferred_element_type=f32)
        scores_ref[to, late:] = lax.dot_general(q_heads, early_keys[block], contract, preferred_element_type=f32)
    q_index = lax.broadcasted_iota(i32, (height, HD), 0) % BLOCK
    k_index = lax.broadcasted_iota(i32, (height, HD), 1)
    ordered = (k_index >= BLOCK) | (k_index <= q_index)
    rate = HD ** (-0.5)
    for block in range(blocks):
        to = slice(block * height, (block + 1) * height)
        scores = scores_ref[to, :]
        scores = jnp.concatenate([jnp.where(ordered, scores[:, :HD], -LARGE), scores[:, HD:]], axis=1)
        exponent = jnp.exp((scores - jnp.max(scores, axis=1, keepdims=True)) * rate)
        weights_ref[to, :] = (exponent * (1.0 / jnp.sum(exponent, axis=1, keepdims=True))).astype(bf16)
    for block in range(blocks):
        at = slice(block * BLOCK, (block + 1) * BLOCK)
        to = slice(block * height, (block + 1) * height)
        context = jnp.dot(weights_ref[to, :late], values[block], preferred_element_type=f32)
        context += jnp.dot(weights_ref[to, late:], early_values[block], preferred_element_type=f32)
        context = context.astype(bf16)
        for h in range(HQ):
            contexts[at, h * HD : (h + 1) * HD] = context[h * BLOCK : (h + 1) * BLOCK, :]
    out_ref[...] = lax.dot_general(
        own_hot, contexts[...], (((0,), (0,)), ((), ())), preferred_element_type=f32
    ).astype(bf16)


def attend(usable, table, lower, queries, early, pieces, capacity, seq_count, slots):
    rows = queries.shape[0]
    blocks = slots // BLOCK
    vmem = pl.BlockSpec(memory_space=pltpu.VMEM)
    count = len(pieces)
    late = count * BLOCK
    total = late + early[0].shape[1]
    height = blocks * HQ * BLOCK
    return pl.pallas_call(
        functools.partial(attention_kernel, count, capacity, seq_count),
        in_specs=[pl.BlockSpec(memory_space=pltpu.SMEM), vmem, vmem, FREE] + [vmem] * (len(early) + count),
        out_shape=jax.ShapeDtypeStruct((rows, QW), bf16),
        scratch_shapes=[
            pltpu.VMEM((blocks, late, 2 * HD), bf16),
            pltpu.VMEM((blocks, late, HD), bf16),
            pltpu.VMEM((slots, QW), bf16),
            pltpu.VMEM((height, total), f32),
            pltpu.VMEM((height, total), bf16),
            pltpu.VMEM((rows, QW), bf16),
            pltpu.SemaphoreType.DMA,
        ],
        compiler_params=params(24),
        name="attention",
    )(usable, table, lower, queries, *early, *pieces)


def rotary(tensor, position):
    half_dim = tensor.shape[-1] // 2
    frequency = jnp.power(
        rope_base, -jnp.arange(half_dim, dtype=jnp.float32) * 2.0 / tensor.shape[-1]
    )
    rotation = position.astype(jnp.float32)[:, None] * frequency[None, :]
    cosine = jnp.cos(rotation)[:, None, :]
    sine_part = jnp.sin(rotation)[:, None, :]
    front_half = tensor[..., :half_dim]
    back_half = tensor[..., half_dim:]
    return jnp.concatenate(
        [front_half * cosine - back_half * sine_part, back_half * cosine + front_half * sine_part],
        axis=-1,
    )


def finish(query_sum, key_sum, value_sum, b_query, b_key, b_value):
    return jnp.concatenate(
        [
            (query_sum + b_query.astype(jnp.float32)).astype(jnp.bfloat16),
            (key_sum + b_key.astype(jnp.float32)).astype(jnp.bfloat16),
            (value_sum + b_value.astype(jnp.float32)).astype(jnp.bfloat16),
        ],
        axis=1,
    )


def project(source_rows, norm_gain, w_query, w_key, w_value, b_query, b_key, b_value):
    widened = source_rows.astype(jnp.float32)
    inverse = lax.rsqrt(jnp.mean(widened * widened, axis=1, keepdims=True) + epsilon)
    query_part = lax.all_gather(w_query, "fsdp", axis=0, tiled=True)
    key_part = lax.all_gather(w_key, "fsdp", axis=0, tiled=True)
    value_part = lax.all_gather(w_value, "fsdp", axis=0, tiled=True)
    gain_part = lax.all_gather(norm_gain, "fsdp", axis=0, tiled=True)
    normed_part = (
        source_rows.astype(jnp.float32) * inverse * gain_part.astype(jnp.float32)
    ).astype(jnp.bfloat16)
    query_sum = jnp.dot(normed_part, query_part, preferred_element_type=jnp.float32)
    key_sum = jnp.dot(normed_part, key_part, preferred_element_type=jnp.float32)
    value_sum = jnp.dot(normed_part, value_part, preferred_element_type=jnp.float32)
    return finish(query_sum, key_sum, value_sum, b_query, b_key, b_value)


def attend_at_host(projected, slot_ids):
    row_count = projected.shape[0]
    query_width = HQ * HD
    queries = projected[:, :query_width].reshape(row_count, HQ, HD)
    keys_raw = projected[:, query_width : query_width + HD]
    values_raw = projected[:, query_width + HD :]
    index_row = jnp.arange(row_count)
    same_slot = slot_ids[:, None] == slot_ids[None, :]
    position = jnp.sum(same_slot & (index_row[None, :] < index_row[:, None]), axis=1)
    allowed = same_slot & (index_row[None, :] <= index_row[:, None])
    query_rot = rotary(queries.astype(jnp.float32), position).astype(jnp.bfloat16)
    key_rot = rotary(keys_raw.astype(jnp.float32)[:, None, :], position)[:, 0, :].astype(
        jnp.bfloat16
    )
    scores = jnp.einsum(
        "qhd,kd->hqk", query_rot, key_rot, preferred_element_type=jnp.float32
    ) * HD ** (-0.5)
    scores = jnp.where(allowed[None, :, :], scores, -jnp.inf)
    largest = jnp.max(scores, axis=-1, keepdims=True)
    exponent = jnp.exp(scores - largest)
    attention = (exponent / jnp.sum(exponent, axis=-1, keepdims=True)).astype(jnp.bfloat16)
    context = jnp.einsum("hqk,kd->qhd", attention, values_raw, preferred_element_type=jnp.float32)
    return context.astype(jnp.bfloat16).reshape(row_count, query_width)


def per_device_exchanged(
    hidden, norm_gain, w_query, w_key, w_value, b_query, b_key, b_value, row_host, row_slot
):
    host_count = lax.axis_size(("dp", "fsdp"))
    source_count = hidden.shape[0]
    capacity = 2 * source_count // host_count
    index_row = jnp.arange(source_count)
    same_host = row_host[:, None] == row_host[None, :]
    row_rank = jnp.sum(same_host & (index_row[None, :] < index_row[:, None]), axis=1)
    slot_index = row_host * capacity + row_rank
    payload = project(hidden, norm_gain, w_query, w_key, w_value, b_query, b_key, b_value)
    payload_width = payload.shape[1]
    outgoing = (
        jnp.zeros((host_count * capacity, payload_width), jnp.bfloat16).at[slot_index].set(payload)
    )
    slot_out = jnp.full((host_count * capacity,), -1, jnp.int32).at[slot_index].set(row_slot)
    arrived, slot_ids = (
        lax.all_to_all(
            outgoing.reshape(host_count, capacity, payload_width),
            ("dp", "fsdp"),
            split_axis=0,
            concat_axis=0,
            tiled=True,
        ),
        lax.all_to_all(
            slot_out.reshape(host_count, capacity),
            ("dp", "fsdp"),
            split_axis=0,
            concat_axis=0,
            tiled=True,
        ),
    )
    arrived = arrived.reshape(host_count * capacity, payload_width)
    slot_ids = slot_ids.reshape(host_count * capacity)
    context = attend_at_host(arrived, slot_ids)
    returned = lax.all_to_all(
        context.reshape(host_count, capacity, context.shape[1]),
        ("dp", "fsdp"),
        split_axis=0,
        concat_axis=0,
        tiled=True,
    )
    return returned.reshape(host_count * capacity, context.shape[1])[slot_index]


def swap_cores(array):
    return lax.ppermute(array, "fsdp", [(0, 1), (1, 0)])


def far(array, shift):
    count = lax.axis_size("dp")
    return lax.ppermute(array, "dp", [(i, (i + shift * 2) % count) for i in range(count)])


def swap_near(array):
    count = lax.axis_size("dp")
    return lax.ppermute(array, "dp", [(i, i ^ 1) for i in range(count)])


def after(array, *others):
    return lax.optimization_barrier((array, *others))[0]


def per_device_stepped(
    hidden, norm_gain, w_query, w_key, w_value, b_query, b_key, b_value, row_host, row_slot
):
    host_count = lax.axis_size(("dp", "fsdp"))
    rows = hidden.shape[0]
    capacity = 2 * rows // host_count
    slots = host_count * capacity
    seq_count = host_count * SLOTS_PER_HOST
    row, core = lax.axis_index("dp"), lax.axis_index("fsdp")
    me = lax.axis_index(("dp", "fsdp"))
    index = jnp.arange(host_count)
    far_row = (row // 2 - index // 4) % 4
    sources = far_row * 4 + ((row % 2) ^ ((index // 2) % 2)) * 2 + (core ^ (index % 2))
    usable = (sources <= me).astype(i32)
    lower = ((sources[None, :] < sources[:, None]) & (usable[None, :] > 0)).astype(f32)
    table = jnp.asarray(rotary_table(2 * rows))
    which = core.reshape(1)

    gain_other = swap_cores(norm_gain)
    w_value_other = swap_cores(w_value)
    w_key_other = swap_cores(w_key)
    facts = facts_of(row_host, row_slot)
    pairs, normed = keys_and_values(
        which, hidden, w_key, w_value, w_key_other, w_value_other,
        norm_gain, gain_other, b_key, b_value, facts,
    )
    w_query_other = swap_cores(after(w_query, w_key_other, w_value_other, gain_other, facts))
    first_half = query_half(True, which, normed, w_query)
    lines = {0: pairs}
    for shift in (2, 3, 1):
        lines[shift] = far(pairs, shift)
    queries = query_half(False, which, normed, w_query_other, first_half, b_query)
    nears = [swap_near(after(lines[shift], queries) if shift in (1, 2) else lines[shift]) for shift in range(4)]
    early_pieces = []
    for shift in (2, 3):
        for here in (lines[shift], nears[shift]):
            early_pieces += [here, swap_cores(here)]
    early = spread_early(usable, table, lower, early_pieces, 8, capacity, seq_count, slots)
    late = []
    for shift in (0, 1):
        for here in (lines[shift], nears[shift]):
            sent = after(here, early[2]) if shift == 1 and here is nears[1] else here
            late += [here, swap_cores(sent)]
    return attend(usable, table, lower, queries, early, late, capacity, seq_count, slots)


def per_device(*args):
    if lax.axis_size("dp") == 8:
        return per_device_stepped(*args)
    return per_device_exchanged(*args)


def solution(mesh):
    return jax.shard_map(
        per_device,
        mesh=mesh,
        in_specs=(
            P(("groups", "dp", "fsdp"), None),
            P("fsdp"),
            P("fsdp", None),
            P("fsdp", None),
            P("fsdp", None),
            P(),
            P(),
            P(),
            P(("groups", "dp", "fsdp")),
            P(("groups", "dp", "fsdp")),
        ),
        out_specs=P(("groups", "dp", "fsdp"), None),
        check_vma=False,
    )
```
